128 devices in a mesh: blk: 16 (over x, z), ma: 8 (over y, core).
Axes of the slice: x: 4, y: 4, z: 4, core: 2. Of those that a mesh axis runs over, the one named last changes fastest.
Arguments:
- weights: bfloat16 [128, 128, 8, 4, 128], P(('blk', 'ma')), may hold values from 0.099609375 to 0.3984375
- offsets: int32 [128, 128, 8, 128], P(('blk', 'ma')), may hold values from 0 to 127
- counts: int32 [128, 128], P(('blk', 'ma')), may hold values from 1 to 8, 576 in all within a row
- block_ids: int32 [128, 128, 8], P(('blk', 'ma')), may hold values from 0 to 127
- m_table: int32 [1536], replicated, may hold values from 0 to 1535, as said below
- legendre: bfloat16 [1536, 1664, 512], P(('blk', 'ma')), as said below
Outputs:
- kappa_band: float32 [4, 512, 4096], P(None, ('blk', 'ma'))
- potential: float32 [4, 512, 4096], P(None, ('blk', 'ma'))
The draws below stay inside these ranges and needn't reach their ends.
Inputs may be any that keep to these rules, and one draw needn't show every extreme that they name: Groups with index below counts[d, e] are live, the others hold no particles; each row sums to (8 + 1) * 128 // 2 and reaches 8. `m_table`: a permutation of 0 to 1535. legendre[j, l, q] is zero for every l below m_table[j].
All inputs are finite; a program needn't handle non-finite values.
Results may differ from the reference program's by a relative error of at most 0.0058.
Values may be sent and summed in bfloat16 or wider, within the bound.
A program may use at most 128 MiB of HBM per device.

```python
import math
import jax
import jax.numpy as jnp
import numpy as np
from jax import lax

NPHI = 4096
L = 1664
NBIN = 4
M_DEV = 12
CAP = 8
CYCLES = 512
M = 1536
BLK_DEV = 128
DEVICES = 128


def draw_offsets(key, part):
    width = 4
    center_key, spread_key, scatter_key, choose_key = jax.random.split(key, 4)
    shape = (DEVICES, DEVICES, CAP, 128)
    centers = jax.random.randint(center_key, (DEVICES, DEVICES, CAP, 1), 0, 128 - width + 1, dtype=jnp.int32)
    spreads = jax.random.randint(spread_key, shape, 0, width, dtype=jnp.int32)
    scattered = jax.random.randint(scatter_key, shape, 0, 128, dtype=jnp.int32)
    in_clump = jax.random.randint(choose_key, shape, 0, 4, dtype=jnp.int32) < 3
    return jnp.where(in_clump, centers + spreads, scattered).astype(jnp.int32)


def draw_m_table(key, part):
    owners = M // M_DEV
    rounds = M_DEV // 2
    subkeys = jax.random.split(key, rounds)
    shuffles = jnp.stack([jax.random.permutation(subkeys[round_index], owners) for round_index in range(rounds)])
    round_ids = jnp.arange(rounds, dtype=jnp.int32)[:, None]
    leading = 2 * round_ids * owners + shuffles
    trailing = (2 * round_ids + 1) * owners + owners - 1 - shuffles
    assignment = jnp.stack([leading, trailing], axis=2)
    return jnp.transpose(assignment, (1, 0, 2)).reshape(M).astype(jnp.int32)


def draw_legendre(key, part):
    orders = draw_m_table(key, part)
    value_key = jax.random.fold_in(key, 7301)
    spread = 0.6 * CYCLES ** (-0.5)
    ramp = jnp.sqrt(jnp.minimum(1.0, (jnp.arange(L, dtype=jnp.float32) + 1.0) / 512.0))[None, :, None]
    values = jax.random.normal(value_key, (M, L, CYCLES), jnp.float32) * spread
    values = values * ramp
    degrees = jnp.arange(L, dtype=jnp.int32)[None, :, None]
    kept = degrees >= orders[:, None, None]
    return jnp.where(kept, values, 0.0).astype(jnp.bfloat16)


def plant(result, key, least, largest):
    index_at = [jax.random.randint(jax.random.fold_in(key, axis), (), 0, length) for axis, length in enumerate(result.shape)]
    longest = result.shape.index(max(result.shape))
    next_to = index_at[:longest] + [(index_at[longest] + 1) % result.shape[longest]] + index_at[longest + 1:]
    return result.at[tuple(index_at)].set(least).at[tuple(next_to)].set(largest)


def steps_of(rng, shape, shards, low, largest):
    def one(dim, parts):
        draws = jax.random.uniform(jax.random.fold_in(jax.random.fold_in(rng, 6), dim), (parts,), jnp.float32, low / len(shards), largest / len(shards))
        return jnp.repeat(jnp.exp(draws), shape[dim] // parts).reshape((-1,) + (1,) * (len(shape) - dim - 1))

    level = one(*shards[0])
    for cut in shards[1:]:
        level = level * one(*cut)
    return level


def split_up(amount, total, most, skew):
    loads = [(1 << 20) // math.isqrt(standing ** skew) + 1 for standing in range(2, amount + 1)]
    surplus, holding = total - most - (amount - 1), [1] * (amount - 1)
    while surplus > 0:
        free = [i for i in range(amount - 1) if holding[i] < most]
        mass, left = sum([loads[i] for i in free]), surplus
        for i in free:
            more = min(most - holding[i], max(1, left * loads[i] // mass), surplus)
            holding[i] = holding[i] + more
            surplus = surplus - more
    return np.array([most] + holding)


def uneven_parts(rng, amount, total, limit, skew):
    if amount == 2:
        one = jax.random.randint(rng, (), max(1, total - limit), min(limit, total - 1) + 1)
        return jnp.stack([one, total - one])
    tallies = jnp.asarray(split_up(amount, total, limit, skew), jnp.int32)
    twos = (amount - 1) // 2
    source_of, taker = tallies[1:1 + 2 * twos:2], tallies[2:2 + 2 * twos:2]
    slack = jnp.minimum(source_of - 1, limit - taker)
    passed = jax.random.randint(jax.random.fold_in(rng, 1), (twos,), 0, 1 << 20) % (slack + 1)
    tallies = tallies.at[1:1 + 2 * twos:2].set(source_of - passed).at[2:2 + 2 * twos:2].set(taker + passed)
    return tallies[jax.random.permutation(jax.random.fold_in(rng, 2), amount)]


def setup_inputs(seed: int = 0) -> dict:
    streams_of = jax.random.split(jax.random.key(seed), 7)
    return {
        "weights": jnp.clip(jnp.exp(math.log(0.3984375) - 1.3862944 * jax.random.uniform(streams_of[0], (DEVICES, DEVICES, CAP, NBIN, 128), jnp.float32) ** steps_of(streams_of[0], (DEVICES, DEVICES, CAP, NBIN, 128), ((0, 128),), -0.2, 0.2)), 0.099609375, 0.3984375).astype(jnp.bfloat16),
        "offsets": draw_offsets(jax.random.fold_in(streams_of[6], 71), 0),
        "counts": jax.vmap(lambda own: uneven_parts(own, DEVICES, (CAP + 1) * DEVICES // 2, CAP, 2))(jax.random.split(streams_of[2], DEVICES)).reshape((DEVICES, DEVICES)).astype(jnp.int32),
        "block_ids": plant(jax.random.randint(streams_of[3], (DEVICES, DEVICES, CAP), 0, BLK_DEV), jax.random.fold_in(streams_of[3], 1), 0, BLK_DEV - 1).astype(jnp.int32),
        "m_table": draw_m_table(jax.random.fold_in(streams_of[6], 71), 0),
        "legendre": draw_legendre(jax.random.fold_in(streams_of[6], 71), 0),
    }


def reference(weights, offsets, counts, block_ids, m_table, legendre):
    live_mask = jnp.arange(CAP, dtype=jnp.int32)[None, None, :] < counts[:, :, None]
    owners = jnp.arange(DEVICES, dtype=jnp.int32)[None, :, None]
    block_start = (owners * BLK_DEV + block_ids) * 128
    flat_index = (block_start[:, :, :, None] + offsets).reshape(-1).astype(jnp.int32)
    masses = jnp.where(live_mask[:, :, :, None, None], weights.astype(jnp.float32), 0.0)
    columns = jnp.transpose(masses, (0, 1, 2, 4, 3)).reshape(-1, NBIN)
    counted = jax.ops.segment_sum(columns, flat_index, num_segments=CYCLES * NPHI)
    convergence = jnp.transpose(counted).reshape(NBIN, CYCLES, NPHI)
    spectrum = jnp.fft.rfft(convergence, axis=-1)
    chosen = jnp.take(spectrum, m_table, axis=2)
    real_part = jnp.real(chosen) / NPHI
    imag_part = jnp.imag(chosen) / NPHI
    parity = jnp.arange(CYCLES, dtype=jnp.int32)[:, None] % 2
    twists = (m_table[None, :] * parity).astype(jnp.float32) * (jnp.pi / NPHI)
    twist_cos = jnp.cos(twists)
    twist_sin = jnp.sin(twists)
    real_turned = real_part * twist_cos + imag_part * twist_sin
    imag_turned = imag_part * twist_cos - real_part * twist_sin
    coefficients = jnp.stack([real_turned, imag_turned], axis=2).astype(jnp.bfloat16)
    coefficients = lax.optimization_barrier(coefficients)
    mode_rows = jnp.transpose(coefficients, (3, 0, 2, 1)).reshape(DEVICES, M_DEV, NBIN, 2, CYCLES)
    tables = legendre.reshape(DEVICES, M_DEV, L, CYCLES)
    degrees = jnp.arange(L, dtype=jnp.float32)
    filter_gain = jnp.where(degrees > 0.5, -20000.0 / jnp.maximum(degrees * (degrees + 1.0), 1.0), 0.0)

    def owner_block(operands):
        basis_block, local_modes = operands
        basis_wide = basis_block.astype(jnp.float32)
        harmonic = jnp.einsum("jlr,jbcr->jbcl", basis_wide, local_modes.astype(jnp.float32), precision=lax.Precision.HIGHEST)
        filtered = jnp.stack([harmonic, harmonic * filter_gain], axis=1).astype(jnp.bfloat16)
        filtered = lax.optimization_barrier(filtered).astype(jnp.float32)
        return jnp.einsum("jlr,jfbcl->jfbcr", basis_wide, filtered, precision=lax.Precision.HIGHEST).astype(jnp.bfloat16)

    synthesis = lax.map(owner_block, (tables, mode_rows)).reshape(M, 2, NBIN, 2, CYCLES)
    values = lax.optimization_barrier(synthesis).astype(jnp.float32)
    real_in = values[:, :, :, 0, :]
    imag_in = values[:, :, :, 1, :]
    turn_cos = jnp.transpose(twist_cos)[:, None, None, :]
    turn_sin = jnp.transpose(twist_sin)[:, None, None, :]
    real_out = real_in * turn_cos - imag_in * turn_sin
    imag_out = real_in * turn_sin + imag_in * turn_cos
    full_real = jnp.zeros((NPHI // 2 + 1, 2, NBIN, CYCLES), jnp.float32).at[m_table].set(real_out)
    full_imag = jnp.zeros((NPHI // 2 + 1, 2, NBIN, CYCLES), jnp.float32).at[m_table].set(imag_out)
    spectrum_out = jnp.transpose(full_real + 1j * full_imag, (1, 2, 3, 0))
    sky_maps = (jnp.fft.irfft(spectrum_out, n=NPHI, axis=-1) * NPHI).astype(jnp.float32)
    return sky_maps[0], sky_maps[1]
```

```python
import math

import jax
import jax.numpy as jnp
import numpy as np
from jax import lax
from jax.experimental import pallas as pl
from jax.experimental.pallas import tpu as pltpu
from jax.sharding import PartitionSpec as P

NPHI = 4096
BANDS = 16
LOCAL = 8
DEVICES = BANDS * LOCAL
CAP = 8
NBIN = 4
SLOTS = 12
DEGREES = 1664
CYCLES = 512
MESH_IDS = pl.DeviceIdType.MESH
bf16 = jnp.bfloat16
f32 = jnp.float32


def nn(a, b):
    return lax.dot_general(a, b, (((1,), (0,)), ((), ())), preferred_element_type=f32)


def nt(a, b):
    return lax.dot_general(a, b, (((1,), (1,)), ((), ())), preferred_element_type=f32)


def two_parts(x):
    high = x.astype(bf16)
    return high, (x - high.astype(f32)).astype(bf16)


def iota(shape, axis):
    return lax.broadcasted_iota(jnp.int32, shape, axis)


def as_one_hot(mask):
    return jnp.where(mask, 1.0, 0.0).astype(bf16)


def tables():
    import ml_dtypes

    def halves(x):
        high = x.astype(np.float32).astype(ml_dtypes.bfloat16)
        low = (x - high.astype(np.float64)).astype(np.float32).astype(ml_dtypes.bfloat16)
        return high, low

    turn = 2.0 * np.pi
    pair, par, quad = np.arange(16), np.arange(2), np.arange(4)
    kb, p, m2 = np.arange(32), np.arange(128), np.arange(64)
    m1 = 2 * pair[None, :] + par[:, None]
    keep = (m2 < 48).astype(np.float64)
    angle = turn * (m1[:, :, None] * kb % 32) / 32
    both = np.stack([np.cos(angle), -np.sin(angle)]) / NPHI
    first = np.einsum("rabk,qs->rabqsk", both, np.eye(4)).reshape(256, 128)
    shift = (quad % 2) / 2.0
    angle = turn * m1[:, :, None, None] * (p[None, :] + shift[:, None]) / NPHI
    twiddle = np.stack([np.cos(angle), np.sin(angle)]).reshape(2, 128, 128)
    angle = turn * (p[:, None] * m2[None, :] % 128) / 128
    c, s = np.cos(angle) * keep, np.sin(angle) * keep
    square = np.array([[c, -s], [s, c]])
    second = np.einsum("iopm,ab->aipobm", square, np.eye(2)).reshape(512, 256)
    angle = np.tile(np.pi * m2 / 128, 2)
    half = np.stack([np.cos(angle), np.sin(angle)])
    half = np.concatenate([half, np.zeros((6, 128))])
    back = []
    for odd in range(2):
        angle = turn * m2[:, None] * (p[None, :] + odd / 2.0) / 128
        value = np.stack([np.cos(angle), np.sin(angle)]) * keep[None, :, None]
        back.append(np.einsum("rmp,ab->ambrp", value, np.eye(2)).reshape(128, 512))
    back = np.stack(back)
    odd = np.arange(2) / 2.0
    angle = turn * m1[None, :, :, None] * (p + odd[:, None, None, None]) / NPHI
    unwind = np.stack([np.cos(angle), np.sin(angle)], axis=1).reshape(2, 2, 2, 16, 1, 128)
    angle = turn * (m1[:, :, None] * kb % 32) / 32
    both = np.stack([np.cos(angle), -np.sin(angle)], axis=1)
    last = np.einsum("aihk,uv->ukaihv", both, np.eye(8)).reshape(256, 512)
    back_parts = halves(back)
    return (
        *halves(first),
        twiddle.astype(np.float32),
        *halves(second),
        half.astype(np.float32),
        np.concatenate(back_parts, axis=1),
        unwind.astype(np.float32),
        *halves(last),
    )


def place(index):
    return (index // LOCAL, lax.rem(index, LOCAL))


def kernel(*refs):
    (
        w_ref, off_ref, ids_ref, mt_ref, leg_ref,
        first_h, first_l, twiddle, second_h, second_l, half, back, unwind, last_h, last_l,
        kappa_ref, potential_ref,
        leg, out1, in1, out2, in2, out3, in3, id1, id2, sel, pick, filt, syn,
        barrier_dummy, leg_sem, send_sem, recv_sem,
    ) = refs
    del barrier_dummy
    band = lax.axis_index("blk")
    local = lax.axis_index("ma")
    me = band * LOCAL + local

    for j in range(SLOTS):
        pltpu.make_async_copy(leg_ref.at[j], leg.at[j], leg_sem.at[j]).start()

    barrier = pltpu.get_barrier_semaphore()

    def greet(i, carry):
        pl.semaphore_signal(
            barrier, inc=1, device_id=place(lax.rem(me + i, DEVICES)), device_id_type=MESH_IDS
        )
        return carry

    lax.fori_loop(1, DEVICES, greet, 0)

    def send(src, dst, k, target):
        pltpu.make_async_remote_copy(
            src_ref=src,
            dst_ref=dst,
            send_sem=send_sem.at[k],
            recv_sem=recv_sem.at[k],
            device_id=target,
            device_id_type=MESH_IDS,
        ).start()

    def settle(ref, k):
        pltpu.make_async_copy(ref, ref, recv_sem.at[k]).wait()

    def sent(ref, k):
        pltpu.make_async_copy(ref, ref, send_sem.at[k]).wait()

    def exchange(out, into, k):
        pltpu.make_async_copy(out.at[me], into.at[me], recv_sem.at[k]).start()

        def one(i, carry):
            t = lax.rem(me + i, DEVICES)
            send(out.at[t], into.at[me], k, place(t))
            return carry

        lax.fori_loop(1, DEVICES, one, 0)

    pl.semaphore_wait(barrier, DEVICES - 1)

    pltpu.make_async_copy(ids_ref.at[local], id1.at[local], recv_sem.at[3]).start()
    for i in range(1, LOCAL):
        t = lax.rem(local + i, LOCAL)
        send(ids_ref.at[t], id1.at[local], 3, (band, t))

    pixel = iota((128, 128), 0)
    group_of_row = iota((32, 128), 0) // 4

    def deposit(i, carry):
        t = lax.rem(me + i, DEVICES)
        w = w_ref[t]
        offs = off_ref[t]
        left = jnp.concatenate(
            [jnp.where(group_of_row == c, w, jnp.zeros_like(w)) for c in range(CAP)], axis=1
        )
        right = jnp.concatenate(
            [as_one_hot(offs[c : c + 1, :] == pixel) for c in range(CAP)], axis=1
        )
        out1[t] = nt(left, right).astype(bf16)
        return t

    t = deposit(0, 0)
    pltpu.make_async_copy(out1.at[t], in1.at[me], recv_sem.at[0]).start()

    def deposit_send(i, carry):
        t = deposit(i, carry)
        send(out1.at[t], in1.at[me], 0, place(t))
        return carry

    lax.fori_loop(1, 64, deposit_send, 0)

    settle(id1, 3)
    pltpu.make_async_copy(id1, id2.at[band], recv_sem.at[4]).start()
    for i in range(1, BANDS):
        t = lax.rem(band + i, BANDS)
        send(id1, id2.at[band], 4, (t, local))

    lax.fori_loop(64, DEVICES, deposit_send, 0)

    lane = iota((1, 2048), 1)
    m2 = lane % 64
    label = jnp.where(m2 < 48, lane // 128 * 2 + lane // 64 % 2 + 32 * m2, -1)
    for j in range(SLOTS):
        pick[pl.ds(128 * j, 128), :] = as_one_hot(mt_ref[:, j : j + 1] == label)

    settle(id2, 4)
    mine = as_one_hot(iota((8, 128), 1) == band * CAP + iota((8, 128), 0))
    ids_cs = nt(mine, id2[...].reshape(DEVICES, 128).astype(bf16)).astype(bf16)
    wide = as_one_hot(iota((128, 4096), 0) == iota((128, 4096), 1) // 32)
    spread = nn(ids_cs, wide)
    lane = iota((8, 4096), 1)
    spread = jnp.where(lane // 4 % 8 == iota((8, 4096), 0), spread, 0.0)
    ids_row = jnp.sum(spread, axis=0, keepdims=True)
    bin_row = (iota((1, 4096), 1) % 4).astype(f32)
    ids_row = jnp.where(ids_row < 0.0, -1.0, ids_row + 128.0 * bin_row)
    for b in range(NBIN):
        rows = (iota((128, 4096), 0) + 128 * b).astype(f32)
        sel[pl.ds(128 * b, 128), :] = as_one_hot(ids_row == rows)

    settle(in1, 0)
    counted = nn(sel[...], in1[...].reshape(4096, 128))

    lefts = []
    for b in range(NBIN):
        high, low = two_parts(counted[128 * b : 128 * b + 128])
        z = nn(first_h[...], high) + nn(first_h[...], low) + nn(first_l[...], high)
        zr, zi = z[:128], z[128:]
        ar = zr * twiddle[0] + zi * twiddle[1]
        ai = zi * twiddle[0] - zr * twiddle[1]
        lefts.append(jnp.concatenate([ar[:64], ai[:64], ar[64:], ai[64:]], axis=1))
    high, low = two_parts(jnp.concatenate(lefts, axis=0))
    x = nn(high, second_h[...]) + nn(low, second_h[...]) + nn(high, second_l[...])
    xr, xi = x[:, :128], x[:, 128:]
    odd = iota((256, 128), 0) % 2 == 1
    c = jnp.where(odd, half[0:1, :], 1.0)
    s = jnp.where(odd, half[1:2, :], 0.0)
    modes = jnp.concatenate([xr * c + xi * s, xi * c - xr * s], axis=0).astype(bf16)
    row, col = iota((512, 512), 0), iota((512, 512), 1)
    origin = row // 4 % 2 * 256 + row % 4 * 64 + row // 32 * 4 + row // 8 % 4
    modes = nn(as_one_hot(col == origin), modes).astype(bf16)
    modes = jnp.concatenate([modes[32 * h : 32 * h + 32] for h in range(16)], axis=1)
    chosen = [nt(modes, pick[pl.ds(128 * j, 128), :]) for j in range(SLOTS)]
    flat2 = out2.reshape(DEVICES * 4, 128)
    for q in range(4):
        block = jnp.concatenate(
            [y[8 * q : 8 * q + 8] for y in chosen] + [jnp.zeros((32, 128), f32)], axis=0
        )
        flat2[pl.ds(q, DEVICES, stride=4), :] = block.T
    exchange(out2, in2, 1)

    for j in range(SLOTS):
        pltpu.make_async_copy(leg_ref.at[j], leg.at[j], leg_sem.at[j]).wait()
    degree = iota((16, DEGREES), 1).astype(f32)
    gain = jnp.where(degree > 0.5, -20000.0 / jnp.maximum(degree * (degree + 1.0), 1.0), 0.0)
    gain = jnp.where(iota((16, DEGREES), 0) // 4 % 2 == 1, gain, 1.0)
    row = iota((192, 128), 0)
    doubled = as_one_hot(iota((192, 128), 1) == row // 16 * 8 + row // 8 % 2 * 4 + row % 4)

    settle(in2, 1)
    mode_rows = nt(doubled, in2[...].reshape(CYCLES, 128).astype(bf16)).astype(bf16)
    for j in range(SLOTS):
        filt[j] = (nt(mode_rows[16 * j : 16 * j + 16], leg[j]) * gain).astype(bf16)
    for j in range(SLOTS):
        syn[pl.ds(16 * j, 16), :] = nn(filt[j], leg[j]).astype(bf16)

    col = iota((512, 512), 1)
    by_quad = as_one_hot(iota((512, 512), 0) == col % 128 * 4 + col // 128)
    maps = nn(syn[...], by_quad)
    flat3 = out3.reshape(DEVICES * 8, 128)
    for h in range(6):
        block = jnp.concatenate(
            [
                maps[16 * j : 16 * j + 16, 128 * q : 128 * q + 128]
                for j in (2 * h, 2 * h + 1)
                for q in range(4)
            ],
            axis=0,
        )
        flat3[pl.ds(h, DEVICES, stride=8), :] = block.T
    for h in range(6, 8):
        flat3[pl.ds(h, DEVICES, stride=8), :] = jnp.zeros((DEVICES, 128), f32)
    exchange(out3, in3, 2)
    settle(in3, 2)

    flat3 = in3.reshape(DEVICES * 8, 128)
    lefts = []
    for h in range(6):
        block = flat3[pl.ds(h, DEVICES, stride=8), :].T.astype(bf16)
        lefts += [block[:64], block[64:]]
    v = nn(jnp.concatenate(lefts, axis=1), pick[...])
    v = (v * jnp.where(iota((1, 2048), 1) == 0, 1.0, 2.0)).astype(bf16)
    rights = [None] * 4
    for odd in range(2):
        left = jnp.concatenate(
            [
                v[16 * q : 16 * q + 16, 128 * h : 128 * h + 128]
                for h in range(16)
                for q in (odd, odd + 2)
            ],
            axis=0,
        )
        g = nn(jnp.concatenate([left, left], axis=1), back[odd])
        g = g.reshape(16, 2, 2, 8, 512)
        parts = ([], [])
        for par in range(2):
            at = 256 * par
            g0c, g0s = g[:, :, 0, :, at : at + 128], g[:, :, 0, :, at + 128 : at + 256]
            g1c, g1s = g[:, :, 1, :, at : at + 128], g[:, :, 1, :, at + 128 : at + 256]
            ur, ui = g0c - g1s, g0s + g1c
            tc, ts = unwind[odd, 0, par][:, None], unwind[odd, 1, par][:, None]
            er, ei = ur * tc - ui * ts, ur * ts + ui * tc
            for k in range(2):
                parts[k].append(er[:, k].reshape(128, 128))
                parts[k].append(ei[:, k].reshape(128, 128))
        for k in range(2):
            rights[odd + 2 * k] = jnp.concatenate(parts[k], axis=0)
    for k in range(2):
        high, low = two_parts(jnp.concatenate(rights[2 * k : 2 * k + 2], axis=1))
        sky = nn(last_h[...], high) + nn(last_h[...], low) + nn(last_l[...], high)
        for q in range(2):
            one = sky[:, 128 * q : 128 * q + 128].reshape(2, 4, 32, 128)
            kappa_ref[:, 2 * k + q] = one[0]
            potential_ref[:, 2 * k + q] = one[1]

    sent(id1.at[pl.ds(0, LOCAL - 1)], 3)
    sent(id2.at[pl.ds(0, BANDS - 1)], 4)
    sent(in1.at[pl.ds(0, DEVICES - 1)], 0)
    sent(in2.at[pl.ds(0, DEVICES - 1)], 1)
    sent(in3.at[pl.ds(0, DEVICES - 1)], 2)


def per_device(weights, offsets, counts, block_ids, m_table, legendre):
    live = lax.broadcasted_iota(jnp.int32, (DEVICES, CAP), 1) < counts[0][:, None]
    ids = jnp.where(live, block_ids[0], -1).astype(f32)
    ids = ids.reshape(BANDS, LOCAL, CAP).transpose(1, 0, 2).reshape(LOCAL, 1, BANDS * CAP)
    constants = [jnp.asarray(t) for t in tables()]
    vmem = pl.BlockSpec(memory_space=pltpu.VMEM)
    hbm = pl.BlockSpec(memory_space=pltpu.HBM)
    shape = jax.ShapeDtypeStruct((NBIN, 4, 32, 128), f32)
    kappa, potential = pl.pallas_call(
        kernel,
        out_shape=(shape, shape),
        in_specs=[vmem] * 4 + [hbm] + [vmem] * len(constants),
        out_specs=(vmem, vmem),
        scratch_shapes=[
            pltpu.VMEM((SLOTS, DEGREES, CYCLES), bf16),
            pltpu.VMEM((DEVICES, 32, 128), bf16),
            pltpu.VMEM((DEVICES, 32, 128), bf16),
            pltpu.VMEM((DEVICES, 4, 128), f32),
            pltpu.VMEM((DEVICES, 4, 128), f32),
            pltpu.VMEM((DEVICES, 8, 128), f32),
            pltpu.VMEM((DEVICES, 8, 128), f32),
            pltpu.VMEM((LOCAL, 1, 128), f32),
            pltpu.VMEM((BANDS, LOCAL, 1, 128), f32),
            pltpu.VMEM((512, 4096), bf16),
            pltpu.VMEM((SLOTS * 128, 2048), bf16),
            pltpu.VMEM((SLOTS, 16, DEGREES), bf16),
            pltpu.VMEM((SLOTS * 16, CYCLES), bf16),
            pltpu.VMEM((8, 128), f32),
            pltpu.SemaphoreType.DMA((SLOTS,)),
            pltpu.SemaphoreType.DMA((5,)),
            pltpu.SemaphoreType.DMA((5,)),
        ],
        compiler_params=pltpu.CompilerParams(
            collective_id=0, has_side_effects=True, vmem_limit_bytes=60 << 20
        ),
        name="deposit_filter",
    )(
        weights[0].reshape(DEVICES, CAP * NBIN, 128),
        offsets[0],
        ids,
        m_table.reshape(DEVICES, SLOTS),
        legendre,
        *constants,
    )
    return kappa.reshape(NBIN, 4, NPHI), potential.reshape(NBIN, 4, NPHI)


def solution(mesh):
    placed = (
        P(("blk", "ma"), None, None, None, None),
        P(("blk", "ma"), None, None, None),
        P(("blk", "ma"), None),
        P(("blk", "ma"), None, None),
        P(),
        P(("blk", "ma"), None, None),
    )
    return jax.shard_map(
        per_device,
        mesh=mesh,
        in_specs=placed,
        out_specs=(P(None, ("blk", "ma"), None), P(None, ("blk", "ma"), None)),
        check_vma=False,
    )
```

```python
import math

import jax
import jax.numpy as jnp
import numpy as np
from jax import lax
from jax.experimental import pallas as pl
from jax.experimental.pallas import tpu as pltpu
from jax.sharding import PartitionSpec as P

NPHI = 4096
BANDS = 16
LOCAL = 8
DEVICES = BANDS * LOCAL
CAP = 8
NBIN = 4
SLOTS = 12
DEGREES = 1664
CYCLES = 512
PART = 32
BATCH = 8
EARLY = 16
MESH_IDS = pl.DeviceIdType.MESH
bf16 = jnp.bfloat16
f32 = jnp.float32


def nn(a, b):
    return lax.dot_general(a, b, (((1,), (0,)), ((), ())), preferred_element_type=f32)


def nt(a, b):
    return lax.dot_general(a, b, (((1,), (1,)), ((), ())), preferred_element_type=f32)


def two_parts(x):
    high = x.astype(bf16)
    return high, (x - high.astype(f32)).astype(bf16)


def iota(shape, axis):
    return lax.broadcasted_iota(jnp.int32, shape, axis)


def as_one_hot(mask):
    return jnp.where(mask, 1.0, 0.0).astype(bf16)


def tables():
    import ml_dtypes

    def halves(x):
        high = x.astype(np.float32).astype(ml_dtypes.bfloat16)
        low = (x - high.astype(np.float64)).astype(np.float32).astype(ml_dtypes.bfloat16)
        return high, low

    turn = 2.0 * np.pi
    pair, par, quad = np.arange(16), np.arange(2), np.arange(4)
    kb, p, m2 = np.arange(32), np.arange(128), np.arange(64)
    m1 = 2 * pair[None, :] + par[:, None]
    keep = (m2 < 48).astype(np.float64)
    angle = turn * (m1[:, :, None] * kb % 32) / 32
    both = np.stack([np.cos(angle), -np.sin(angle)]) / NPHI
    first = np.einsum("rabk,qs->rabqsk", both, np.eye(4)).reshape(256, 128)
    shift = (quad % 2) / 2.0
    angle = turn * m1[:, :, None, None] * (p[None, :] + shift[:, None]) / NPHI
    twiddle = np.stack([np.cos(angle), np.sin(angle)]).reshape(2, 128, 128)
    angle = turn * (p[:, None] * m2[None, :] % 128) / 128
    c, s = np.cos(angle) * keep, np.sin(angle) * keep
    square = np.array([[c, -s], [s, c]])
    second = np.einsum("iopm,ab->aipobm", square, np.eye(2)).reshape(512, 256)
    angle = np.tile(np.pi * m2 / 128, 2)
    half = np.stack([np.cos(angle), np.sin(angle)])
    half = np.concatenate([half, np.zeros((6, 128))])
    back = []
    for odd in range(2):
        angle = turn * m2[:, None] * (p[None, :] + odd / 2.0) / 128
        value = np.stack([np.cos(angle), np.sin(angle)]) * keep[None, :, None]
        back.append(np.einsum("rmp,ab->ambrp", value, np.eye(2)).reshape(128, 512))
    back = np.stack(back)
    odd = np.arange(2) / 2.0
    angle = turn * m1[None, :, :, None] * (p + odd[:, None, None, None]) / NPHI
    unwind = np.stack([np.cos(angle), np.sin(angle)], axis=1).reshape(2, 2, 2, 16, 1, 128)
    angle = turn * (m1[:, :, None] * kb % 32) / 32
    both = np.stack([np.cos(angle), -np.sin(angle)], axis=1)
    last = np.einsum("aihk,uv->ukaihv", both, np.eye(8)).reshape(256, 512)
    back_parts = halves(back)
    return (
        *halves(first),
        twiddle.astype(np.float32),
        *halves(second),
        half.astype(np.float32),
        np.concatenate(back_parts, axis=1),
        unwind.astype(np.float32),
        *halves(last),
    )


def place(index):
    return (index // LOCAL, lax.rem(index, LOCAL))


def kernel(*refs):
    (
        w_ref, off_ref, blocks_ref, counts_ref, orders_ref, leg_ref, *constants,
    ) = refs[:16]
    kappa_ref, potential_ref = refs[16:18]
    held = refs[18:28]
    first_h, first_l, twiddle, second_h, second_l, half, back, unwind, last_h, last_l = held
    (
        leg, out1, in1, out2, in2, out3, in3, id0, id1, idx, id2, sel, pick, filt, syn,
        const_sem, leg_sem, send_sem, recv_sem, part_sem,
    ) = refs[28:]
    band = lax.axis_index("blk")
    local = lax.axis_index("ma")
    me = band * LOCAL + local

    barrier = pltpu.get_barrier_semaphore()

    def greet(i, carry):
        pl.semaphore_signal(
            barrier, inc=1, device_id=place(lax.rem(me + i, DEVICES)), device_id_type=MESH_IDS
        )
        return carry

    lax.fori_loop(1, DEVICES, greet, 0)

    def send(src, dst, k, target):
        pltpu.make_async_remote_copy(
            src_ref=src,
            dst_ref=dst,
            send_sem=send_sem.at[k],
            recv_sem=recv_sem.at[k],
            device_id=target,
            device_id_type=MESH_IDS,
        ).start()

    def settle(ref, k):
        pltpu.make_async_copy(ref, ref, recv_sem.at[k]).wait()

    def sent(ref, k):
        pltpu.make_async_copy(ref, ref, send_sem.at[k]).wait()

    def exchange(out, into, k):
        pltpu.make_async_copy(out.at[me], into.at[me], recv_sem.at[k]).start()

        def one(i, carry):
            t = lax.rem(me + i, DEVICES)
            send(out.at[t], into.at[me], k, place(t))
            return carry

        lax.fori_loop(1, DEVICES, one, 0)

    for n in range(10):
        pltpu.make_async_copy(constants[n], held[n], const_sem.at[n]).start()
    for j in range(SLOTS):
        pltpu.make_async_copy(leg_ref.at[j], leg.at[j], leg_sem.at[j]).start()

    pixel = iota((128, 128), 0).astype(f32).astype(bf16)
    group_of_row = iota((32, 128), 0) // 4

    def deposit(i, carry):
        t = lax.rem(me + i, DEVICES)
        w = w_ref[t]
        offs = off_ref[t].astype(f32).astype(bf16)
        left = jnp.concatenate(
            [jnp.where(group_of_row == c, w, jnp.zeros_like(w)) for c in range(CAP)], axis=1
        )
        one, zero = jnp.ones((), bf16), jnp.zeros((), bf16)
        right = jnp.concatenate(
            [jnp.where(offs[c : c + 1, :] == pixel, one, zero) for c in range(CAP)], axis=1
        )
        out1[i] = nt(left, right).astype(bf16)
        return carry

    def send_part(i, k):
        pltpu.make_async_remote_copy(
            src_ref=out1.at[i],
            dst_ref=in1.at[i],
            send_sem=send_sem.at[0],
            recv_sem=part_sem.at[k],
            device_id=place(lax.rem(me + i, DEVICES)),
            device_id_type=MESH_IDS,
        ).start()

    live = iota((CAP, DEVICES), 0) < counts_ref[...]
    id0[...] = jnp.where(live, blocks_ref[...], -1).astype(f32)
    lax.fori_loop(0, EARLY, deposit, 0, unroll=4)
    pl.semaphore_wait(barrier, DEVICES - 1)

    pltpu.make_async_copy(id0, id1.at[local], recv_sem.at[3]).start()
    for i in range(1, LOCAL):
        send(id0, id1.at[local], 3, (band, lax.rem(local + i, LOCAL)))

    pltpu.make_async_copy(out1.at[0], in1.at[0], part_sem.at[0]).start()

    def early(i, carry):
        send_part(i, 0)
        return carry

    lax.fori_loop(1, EARLY, early, 0)

    def deposit_send(k):
        def step(n, carry):
            for u in range(BATCH):
                deposit(n * BATCH + u, carry)
            for u in range(BATCH):
                send_part(n * BATCH + u, k)
            return carry

        return step

    lax.fori_loop(EARLY // BATCH, PART // BATCH, deposit_send(0), 0)
    lax.fori_loop(1 * PART // BATCH, 2 * PART // BATCH, deposit_send(1), 0)

    settle(id1, 3)
    column = as_one_hot(iota((BANDS, DEVICES), 1) == iota((BANDS, DEVICES), 0) * LOCAL + local)
    every = id1[...].reshape(LOCAL * CAP, DEVICES).astype(bf16)
    every = nt(column, jnp.concatenate([every, every], axis=0))
    for i in range(BANDS):
        idx[i] = every[i : i + 1]
    pltpu.make_async_copy(idx.at[band], id2.at[band], recv_sem.at[4]).start()
    for i in range(1, BANDS):
        t = lax.rem(band + i, BANDS)
        send(idx.at[t], id2.at[band], 4, (t, local))

    lax.fori_loop(2 * PART // BATCH, 3 * PART // BATCH, deposit_send(2), 0)
    lax.fori_loop(3 * PART // BATCH, 4 * PART // BATCH, deposit_send(3), 0)

    slot = iota((DEVICES, 1536), 1)
    owner = (slot * 5462) >> 16
    orders = jnp.broadcast_to(orders_ref[...].reshape(1, 1536), (DEVICES, 1536)).astype(f32)
    orders = jnp.where(owner == iota((DEVICES, 1536), 0), orders, 0.0)
    slot = iota((16, 1536), 1)
    which = as_one_hot(slot - ((slot * 5462) >> 16) * SLOTS == iota((16, 1536), 0))
    high, low = two_parts(orders)
    orders = nt(high, which) + nt(low, which)

    lane = iota((1, 2048), 1)
    m2 = lane % 64
    label = jnp.where(m2 < 48, lane // 128 * 2 + lane // 64 % 2 + 32 * m2, -1).astype(f32)
    for j in range(SLOTS):
        pick[pl.ds(128 * j, 128), :] = as_one_hot(orders[:, j : j + 1] == label)

    settle(id2, 4)
    at = iota((128, 4096), 1)
    source = me + DEVICES - (at >> 5)
    wide = as_one_hot(iota((128, 4096), 0) == (source & 7) * CAP + ((at >> 2) & 7))
    spread = nn(id2[...].reshape(BANDS, 128).astype(bf16), wide)
    at = iota((BANDS, 4096), 1)
    source = me + DEVICES - (at >> 5)
    spread = jnp.where(((source >> 3) & 15) == iota((BANDS, 4096), 0), spread, 0.0)
    ids_row = jnp.sum(spread, axis=0, keepdims=True)
    bin_row = (iota((1, 4096), 1) & 3).astype(f32)
    ids_row = jnp.where(ids_row < 0.0, -1.0, ids_row + 128.0 * bin_row)
    for b in range(NBIN):
        rows = (iota((128, 4096), 0) + 128 * b).astype(f32)
        sel[pl.ds(128 * b, 128), :] = as_one_hot(ids_row == rows)

    for n in range(10):
        pltpu.make_async_copy(constants[n], held[n], const_sem.at[n]).wait()
    counted = None
    for k in range(4):
        piece = in1.at[pl.ds(PART * k, PART)]
        pltpu.make_async_copy(piece, piece, part_sem.at[k]).wait()
        term = nn(sel[:, 1024 * k : 1024 * k + 1024], piece[...].reshape(1024, 128))
        counted = term if counted is None else counted + term

    lefts = []
    for b in range(NBIN):
        high, low = two_parts(counted[128 * b : 128 * b + 128])
        z = nn(first_h[...], high) + nn(first_h[...], low) + nn(first_l[...], high)
        zr, zi = z[:128], z[128:]
        ar = zr * twiddle[0] + zi * twiddle[1]
        ai = zi * twiddle[0] - zr * twiddle[1]
        lefts.append(jnp.concatenate([ar[:64], ai[:64], ar[64:], ai[64:]], axis=1))
    high, low = two_parts(jnp.concatenate(lefts, axis=0))
    x = nn(high, second_h[...]) + nn(low, second_h[...]) + nn(high, second_l[...])
    xr, xi = x[:, :128], x[:, 128:]
    odd = iota((256, 128), 0) % 2 == 1
    c = jnp.where(odd, half[0:1, :], 1.0)
    s = jnp.where(odd, half[1:2, :], 0.0)
    modes = jnp.concatenate([xr * c + xi * s, xi * c - xr * s], axis=0).astype(bf16)
    row, col = iota((512, 512), 0), iota((512, 512), 1)
    origin = row // 4 % 2 * 256 + row % 4 * 64 + row // 32 * 4 + row // 8 % 4
    modes = nn(as_one_hot(col == origin), modes).astype(bf16)
    modes = jnp.concatenate([modes[32 * h : 32 * h + 32] for h in range(16)], axis=1)
    chosen = [nt(modes, pick[pl.ds(128 * j, 128), :]) for j in range(SLOTS)]
    flat2 = out2.reshape(DEVICES * 4, 128)
    for q in range(4):
        block = jnp.concatenate(
            [y[8 * q : 8 * q + 8] for y in chosen] + [jnp.zeros((32, 128), f32)], axis=0
        )
        flat2[pl.ds(q, DEVICES, stride=4), :] = block.T
    exchange(out2, in2, 1)

    for j in range(SLOTS):
        pltpu.make_async_copy(leg_ref.at[j], leg.at[j], leg_sem.at[j]).wait()
    degree = iota((16, DEGREES), 1).astype(f32)
    gain = jnp.where(degree > 0.5, -20000.0 / jnp.maximum(degree * (degree + 1.0), 1.0), 0.0)
    gain = jnp.where(iota((16, DEGREES), 0) // 4 % 2 == 1, gain, 1.0)
    row = iota((192, 128), 0)
    doubled = as_one_hot(iota((192, 128), 1) == row // 16 * 8 + row // 8 % 2 * 4 + row % 4)

    settle(in2, 1)
    mode_rows = nt(doubled, in2[...].reshape(CYCLES, 128).astype(bf16)).astype(bf16)
    for j in range(SLOTS):
        filt[j] = (nt(mode_rows[16 * j : 16 * j + 16], leg[j]) * gain).astype(bf16)
    for j in range(SLOTS):
        syn[pl.ds(16 * j, 16), :] = nn(filt[j], leg[j]).astype(bf16)

    col = iota((512, 512), 1)
    by_quad = as_one_hot(iota((512, 512), 0) == col % 128 * 4 + col // 128)
    maps = nn(syn[...], by_quad)
    flat3 = out3.reshape(DEVICES * 8, 128)
    for h in range(6):
        block = jnp.concatenate(
            [
                maps[16 * j : 16 * j + 16, 128 * q : 128 * q + 128]
                for j in (2 * h, 2 * h + 1)
                for q in range(4)
            ],
            axis=0,
        )
        flat3[pl.ds(h, DEVICES, stride=8), :] = block.T
    for h in range(6, 8):
        flat3[pl.ds(h, DEVICES, stride=8), :] = jnp.zeros((DEVICES, 128), f32)
    exchange(out3, in3, 2)
    settle(in3, 2)

    flat3 = in3.reshape(DEVICES * 8, 128)
    lefts = []
    for h in range(6):
        block = flat3[pl.ds(h, DEVICES, stride=8), :].T.astype(bf16)
        lefts += [block[:64], block[64:]]
    v = nn(jnp.concatenate(lefts, axis=1), pick[...])
    v = (v * jnp.where(iota((1, 2048), 1) == 0, 1.0, 2.0)).astype(bf16)
    rights = [None] * 4
    for odd in range(2):
        left = jnp.concatenate(
            [
                v[16 * q : 16 * q + 16, 128 * h : 128 * h + 128]
                for h in range(16)
                for q in (odd, odd + 2)
            ],
            axis=0,
        )
        g = nn(jnp.concatenate([left, left], axis=1), back[odd])
        g = g.reshape(16, 2, 2, 8, 512)
        parts = ([], [])
        for par in range(2):
            at = 256 * par
            g0c, g0s = g[:, :, 0, :, at : at + 128], g[:, :, 0, :, at + 128 : at + 256]
            g1c, g1s = g[:, :, 1, :, at : at + 128], g[:, :, 1, :, at + 128 : at + 256]
            ur, ui = g0c - g1s, g0s + g1c
            tc, ts = unwind[odd, 0, par][:, None], unwind[odd, 1, par][:, None]
            er, ei = ur * tc - ui * ts, ur * ts + ui * tc
            for k in range(2):
                parts[k].append(er[:, k].reshape(128, 128))
                parts[k].append(ei[:, k].reshape(128, 128))
        for k in range(2):
            rights[odd + 2 * k] = jnp.concatenate(parts[k], axis=0)
    for k in range(2):
        high, low = two_parts(jnp.concatenate(rights[2 * k : 2 * k + 2], axis=1))
        sky = nn(last_h[...], high) + nn(last_h[...], low) + nn(last_l[...], high)
        for q in range(2):
            one = sky[:, 128 * q : 128 * q + 128].reshape(2, 4, 32, 128)
            for b in range(NBIN):
                kappa_ref[b, pl.ds(2 * k + q, 32, stride=4), :] = one[0, b]
                potential_ref[b, pl.ds(2 * k + q, 32, stride=4), :] = one[1, b]

    sent(id1.at[pl.ds(0, LOCAL - 1)], 3)
    sent(id2.at[pl.ds(0, BANDS - 1)], 4)
    sent(in1.at[pl.ds(0, DEVICES - 1)], 0)
    sent(in2.at[pl.ds(0, DEVICES - 1)], 1)
    sent(in3.at[pl.ds(0, DEVICES - 1)], 2)


def hand_over(kappa, potential, kappa_out, potential_out, sems):
    copies = [
        pltpu.make_async_copy(kappa, kappa_out, sems.at[0]),
        pltpu.make_async_copy(potential, potential_out, sems.at[1]),
    ]
    for copy in copies:
        copy.start()
    for copy in copies:
        copy.wait()


def per_device(weights, offsets, counts, block_ids, m_table, legendre):
    constants = [jnp.asarray(t) for t in tables()]
    vmem = pl.BlockSpec(memory_space=pltpu.VMEM)
    hbm = pl.BlockSpec(memory_space=pltpu.HBM)
    shape = jax.ShapeDtypeStruct((NBIN, 128, 128), f32)
    kappa, potential = pl.pallas_call(
        kernel,
        out_shape=(shape, shape),
        in_specs=[vmem] * 5 + [hbm] * 11,
        out_specs=(vmem, vmem),
        scratch_shapes=[
            *[pltpu.VMEM(t.shape, t.dtype) for t in constants],
            pltpu.VMEM((SLOTS, DEGREES, CYCLES), bf16),
            pltpu.VMEM((DEVICES, 32, 128), bf16),
            pltpu.VMEM((DEVICES, 32, 128), bf16),
            pltpu.VMEM((DEVICES, 4, 128), f32),
            pltpu.VMEM((DEVICES, 4, 128), f32),
            pltpu.VMEM((DEVICES, 8, 128), f32),
            pltpu.VMEM((DEVICES, 8, 128), f32),
            pltpu.VMEM((CAP, DEVICES), f32),
            pltpu.VMEM((LOCAL, CAP, DEVICES), f32),
            pltpu.VMEM((BANDS, 1, 128), f32),
            pltpu.VMEM((BANDS, 1, 128), f32),
            pltpu.VMEM((512, 4096), bf16),
            pltpu.VMEM((SLOTS * 128, 2048), bf16),
            pltpu.VMEM((SLOTS, 16, DEGREES), bf16),
            pltpu.VMEM((SLOTS * 16, CYCLES), bf16),
            pltpu.SemaphoreType.DMA((10,)),
            pltpu.SemaphoreType.DMA((SLOTS,)),
            pltpu.SemaphoreType.DMA((5,)),
            pltpu.SemaphoreType.DMA((5,)),
            pltpu.SemaphoreType.DMA((4,)),
        ],
        compiler_params=pltpu.CompilerParams(
            collective_id=0, has_side_effects=True, vmem_limit_bytes=60 << 20
        ),
        name="deposit_filter",
    )(
        weights[0].reshape(DEVICES, CAP * NBIN, 128),
        offsets[0],
        jnp.swapaxes(block_ids, 1, 2).reshape(CAP, DEVICES),
        counts,
        m_table,
        legendre,
        *constants,
    )
    kappa, potential = pl.pallas_call(
        hand_over,
        out_shape=(shape, shape),
        in_specs=[vmem, vmem],
        out_specs=(hbm, hbm),
        scratch_shapes=[pltpu.SemaphoreType.DMA((2,))],
        name="hand_over",
    )(kappa, potential)
    maps = [x.reshape(NBIN, 32, 4, 128).transpose(0, 2, 1, 3) for x in (kappa, potential)]
    return tuple(x.reshape(NBIN, 4, NPHI) for x in maps)


def solution(mesh):
    placed = (
        P(("blk", "ma"), None, None, None, None),
        P(("blk", "ma"), None, None, None),
        P(("blk", "ma"), None),
        P(("blk", "ma"), None, None),
        P(),
        P(("blk", "ma"), None, None),
    )
    return jax.shard_map(
        per_device,
        mesh=mesh,
        in_specs=placed,
        out_specs=(P(None, ("blk", "ma"), None), P(None, ("blk", "ma"), None)),
        check_vma=False,
    )
```

```python
import math

import jax
import jax.numpy as jnp
import numpy as np
from jax import lax
from jax.experimental import pallas as pl
from jax.experimental.pallas import tpu as pltpu
from jax.sharding import PartitionSpec as P

NPHI = 4096
BANDS = 16
LOCAL = 8
DEVICES = BANDS * LOCAL
CHIPS = DEVICES // 2
CAP = 8
NBIN = 4
SLOTS = 12
DEGREES = 1664
CYCLES = 512
PART = 32
BATCH = 8
STRIDE = 27
EARLY = 16
MESH_IDS = pl.DeviceIdType.MESH
bf16 = jnp.bfloat16
f32 = jnp.float32


def nn(a, b):
    return lax.dot_general(a, b, (((1,), (0,)), ((), ())), preferred_element_type=f32)


def nt(a, b):
    return lax.dot_general(a, b, (((1,), (1,)), ((), ())), preferred_element_type=f32)


def two_parts(x):
    high = x.astype(bf16)
    return high, (x - high.astype(f32)).astype(bf16)


def iota(shape, axis):
    return lax.broadcasted_iota(jnp.int32, shape, axis)


def as_one_hot(mask):
    return jnp.where(mask, 1.0, 0.0).astype(bf16)


def tables():
    import ml_dtypes

    def halves(x):
        high = x.astype(np.float32).astype(ml_dtypes.bfloat16)
        low = (x - high.astype(np.float64)).astype(np.float32).astype(ml_dtypes.bfloat16)
        return high, low

    turn = 2.0 * np.pi
    pair, par, quad = np.arange(16), np.arange(2), np.arange(4)
    kb, p, m2 = np.arange(32), np.arange(128), np.arange(64)
    m1 = 2 * pair[None, :] + par[:, None]
    keep = (m2 < 48).astype(np.float64)
    angle = turn * (m1[:, :, None] * kb % 32) / 32
    both = np.stack([np.cos(angle), -np.sin(angle)]) / NPHI
    first = np.einsum("rabk,qs->rabqsk", both, np.eye(4)).reshape(256, 128)
    shift = (quad % 2) / 2.0
    angle = turn * m1[:, :, None, None] * (p[None, :] + shift[:, None]) / NPHI
    twiddle = np.stack([np.cos(angle), np.sin(angle)]).reshape(2, 128, 128)
    angle = turn * (p[:, None] * m2[None, :] % 128) / 128
    c, s = np.cos(angle) * keep, np.sin(angle) * keep
    square = np.array([[c, -s], [s, c]])
    second = np.einsum("iopm,ab->aipobm", square, np.eye(2)).reshape(512, 256)
    angle = np.tile(np.pi * m2 / 128, 2)
    half = np.stack([np.cos(angle), np.sin(angle)])
    half = np.concatenate([half, np.zeros((6, 128))])
    back = []
    for odd in range(2):
        angle = turn * m2[:, None] * (p[None, :] + odd / 2.0) / 128
        value = np.stack([np.cos(angle), np.sin(angle)]) * keep[None, :, None]
        back.append(np.einsum("rmp,ab->ambrp", value, np.eye(2)).reshape(128, 512))
    back = np.stack(back)
    odd = np.arange(2) / 2.0
    angle = turn * m1[None, :, :, None] * (p + odd[:, None, None, None]) / NPHI
    unwind = np.stack([np.cos(angle), np.sin(angle)], axis=1).reshape(2, 2, 2, 16, 1, 128)
    angle = turn * (m1[:, :, None] * kb % 32) / 32
    both = np.stack([np.cos(angle), -np.sin(angle)], axis=1)
    last = np.einsum("aihk,uv->ukaihv", both, np.eye(8)).reshape(256, 512)
    back_parts = halves(back)
    return (
        *halves(first),
        twiddle.astype(np.float32),
        *halves(second),
        half.astype(np.float32),
        np.concatenate(back_parts, axis=1),
        unwind.astype(np.float32),
        *halves(last),
    )


def place(index):
    return (index // LOCAL, lax.rem(index, LOCAL))


def kernel(*refs):
    (
        w_ref, off_ref, blocks_ref, counts_ref, orders_ref, leg_ref, *constants,
    ) = refs[:16]
    kappa_ref, potential_ref = refs[16:18]
    held = refs[18:28]
    first_h, first_l, twiddle, second_h, second_l, half, back, unwind, last_h, last_l = held
    (
        leg, out1, in1, near2, out2, in2, near3, got3, out3, in3, stage, id0, id1, idx, id2, sel, pick, filt, syn,
        const_sem, leg_sem, send_sem, recv_sem, part_sem,
    ) = refs[28:]
    band = lax.axis_index("blk")
    local = lax.axis_index("ma")
    me = band * LOCAL + local
    core = lax.rem(local, 2)
    chip = me // 2
    sibling = (band, local + 1 - 2 * core)

    barrier = pltpu.get_barrier_semaphore()

    def greet(i, carry):
        pl.semaphore_signal(
            barrier, inc=1, device_id=place(lax.rem(me + i, DEVICES)), device_id_type=MESH_IDS
        )
        return carry

    lax.fori_loop(1, DEVICES, greet, 0)

    def send(src, dst, k, target):
        pltpu.make_async_remote_copy(
            src_ref=src,
            dst_ref=dst,
            send_sem=send_sem.at[k],
            recv_sem=recv_sem.at[k],
            device_id=target,
            device_id_type=MESH_IDS,
        ).start()

    def settle(ref, k):
        pltpu.make_async_copy(ref, ref, recv_sem.at[k]).wait()

    def sent(ref, k):
        pltpu.make_async_copy(ref, ref, send_sem.at[k]).wait()

    def exchange(out, into, k):
        pltpu.make_async_copy(out.at[chip], into.at[chip], recv_sem.at[k]).start()

        def one(i, carry):
            t = lax.rem(chip + i, CHIPS)
            send(out.at[t], into.at[chip], k, place(2 * t + core))
            return carry

        lax.fori_loop(1, CHIPS, one, 0)

    for n in range(10):
        pltpu.make_async_copy(constants[n], held[n], const_sem.at[n]).start()
    for j in range(SLOTS):
        pltpu.make_async_copy(leg_ref.at[j], leg.at[j], leg_sem.at[j]).start()

    pixel = iota((128, 128), 0).astype(f32).astype(bf16)
    group_of_row = iota((32, 128), 0) // 4

    def target(i):
        step = lax.rem(i * STRIDE, DEVICES)
        return lax.rem(band + step // LOCAL, BANDS), lax.rem(local + lax.rem(step, LOCAL), LOCAL)

    def deposit(i, carry):
        t = target(i)
        t = t[0] * LOCAL + t[1]
        w = w_ref[t]
        offs = off_ref[t].astype(f32).astype(bf16)
        left = jnp.concatenate(
            [jnp.where(group_of_row == c, w, jnp.zeros_like(w)) for c in range(CAP)], axis=1
        )
        one, zero = jnp.ones((), bf16), jnp.zeros((), bf16)
        right = jnp.concatenate(
            [jnp.where(offs[c : c + 1, :] == pixel, one, zero) for c in range(CAP)], axis=1
        )
        out1[i] = nt(left, right).astype(bf16)
        return carry

    def send_part(i, k):
        pltpu.make_async_remote_copy(
            src_ref=out1.at[i],
            dst_ref=in1.at[i],
            send_sem=send_sem.at[0],
            recv_sem=part_sem.at[k],
            device_id=target(i),
            device_id_type=MESH_IDS,
        ).start()

    live = iota((CAP, DEVICES), 0) < counts_ref[...]
    id0[...] = jnp.where(live, blocks_ref[...], -1).astype(f32)
    lax.fori_loop(0, EARLY, deposit, 0, unroll=4)
    pl.semaphore_wait(barrier, DEVICES - 1)

    pltpu.make_async_copy(id0, id1.at[local], recv_sem.at[3]).start()
    for i in range(1, LOCAL):
        send(id0, id1.at[local], 3, (band, lax.rem(local + i, LOCAL)))

    pltpu.make_async_copy(out1.at[0], in1.at[0], part_sem.at[0]).start()

    def early(i, carry):
        send_part(i, 0)
        return carry

    lax.fori_loop(1, EARLY, early, 0)

    def deposit_send(k):
        def step(n, carry):
            for u in range(BATCH):
                deposit(n * BATCH + u, carry)
            for u in range(BATCH):
                send_part(n * BATCH + u, k)
            return carry

        return step

    lax.fori_loop(EARLY // BATCH, PART // BATCH, deposit_send(0), 0)
    lax.fori_loop(1 * PART // BATCH, 2 * PART // BATCH, deposit_send(1), 0)

    settle(id1, 3)
    column = as_one_hot(iota((BANDS, DEVICES), 1) == iota((BANDS, DEVICES), 0) * LOCAL + local)
    every = id1[...].reshape(LOCAL * CAP, DEVICES).astype(bf16)
    every = nt(column, jnp.concatenate([every, every], axis=0))
    for i in range(BANDS):
        idx[i] = every[i : i + 1]
    pltpu.make_async_copy(idx.at[band], id2.at[band], recv_sem.at[4]).start()
    for i in range(1, BANDS):
        t = lax.rem(band + i, BANDS)
        send(idx.at[t], id2.at[band], 4, (t, local))

    lax.fori_loop(2 * PART // BATCH, 3 * PART // BATCH, deposit_send(2), 0)
    lax.fori_loop(3 * PART // BATCH, 4 * PART // BATCH, deposit_send(3), 0)

    slot = iota((DEVICES, 1536), 1)
    owner = (slot * 5462) >> 16
    orders = jnp.broadcast_to(orders_ref[...].reshape(1, 1536), (DEVICES, 1536)).astype(f32)
    row = iota((DEVICES, 1536), 0)
    device = 2 * (row & 63) + jnp.where(row < CHIPS, core, 1 - core)
    orders = jnp.where(owner == device, orders, 0.0)
    slot = iota((16, 1536), 1)
    which = as_one_hot(slot - ((slot * 5462) >> 16) * SLOTS == iota((16, 1536), 0))
    high, low = two_parts(orders)
    orders = nt(high, which) + nt(low, which)

    stage[...] = jnp.zeros_like(stage)

    lane = iota((1, 2048), 1)
    m2 = lane % 64
    label = jnp.where(m2 < 48, lane // 128 * 2 + lane // 64 % 2 + 32 * m2, -1).astype(f32)
    for j in range(SLOTS):
        pick[pl.ds(128 * j, 128), :] = as_one_hot(orders[:, j : j + 1] == label)

    settle(id2, 4)
    at = iota((128, 4096), 1)
    step = (at >> 5) * STRIDE & 127
    wide = as_one_hot(iota((128, 4096), 0) == (local - step & 7) * CAP + ((at >> 2) & 7))
    spread = nn(id2[...].reshape(BANDS, 128).astype(bf16), wide)
    at = iota((BANDS, 4096), 1)
    step = (at >> 5) * STRIDE & 127
    spread = jnp.where((band - (step >> 3) & 15) == iota((BANDS, 4096), 0), spread, 0.0)
    ids_row = jnp.sum(spread, axis=0, keepdims=True)
    bin_row = (iota((1, 4096), 1) & 3).astype(f32)
    ids_row = jnp.where(ids_row < 0.0, -1.0, ids_row + 128.0 * bin_row)
    for b in range(NBIN):
        rows = (iota((128, 4096), 0) + 128 * b).astype(f32)
        sel[pl.ds(128 * b, 128), :] = as_one_hot(ids_row == rows)

    for n in range(10):
        pltpu.make_async_copy(constants[n], held[n], const_sem.at[n]).wait()
    counted = None
    for k in range(4):
        piece = in1.at[pl.ds(PART * k, PART)]
        pltpu.make_async_copy(piece, piece, part_sem.at[k]).wait()
        term = nn(sel[:, 1024 * k : 1024 * k + 1024], piece[...].reshape(1024, 128))
        counted = term if counted is None else counted + term

    lefts = []
    high, low = two_parts(
        jnp.concatenate([counted[128 * b : 128 * b + 128] for b in range(NBIN)], axis=1)
    )
    both = jnp.concatenate([first_h[...], first_l[...]], axis=1)
    every = nn(both, jnp.concatenate([high, high], axis=0)) + nn(first_h[...], low)
    for b in range(NBIN):
        z = every[:, 128 * b : 128 * b + 128]
        zr, zi = z[:128], z[128:]
        ar = zr * twiddle[0] + zi * twiddle[1]
        ai = zi * twiddle[0] - zr * twiddle[1]
        lefts.append(jnp.concatenate([ar[:64], ai[:64], ar[64:], ai[64:]], axis=1))
    high, low = two_parts(jnp.concatenate(lefts, axis=0))
    x = nn(high, second_h[...]) + nn(low, second_h[...]) + nn(high, second_l[...])
    xr, xi = x[:, :128], x[:, 128:]
    odd = iota((256, 128), 0) % 2 == 1
    c = jnp.where(odd, half[0:1, :], 1.0)
    s = jnp.where(odd, half[1:2, :], 0.0)
    modes = jnp.concatenate([xr * c + xi * s, xi * c - xr * s], axis=0).astype(bf16)
    row, col = iota((512, 512), 0), iota((512, 512), 1)
    origin = row // 4 % 2 * 256 + row % 4 * 64 + row // 32 * 4 + row // 8 % 4
    modes = nn(as_one_hot(col == origin), modes).astype(bf16)
    modes = jnp.concatenate([modes[32 * h : 32 * h + 32] for h in range(16)], axis=1)
    chosen = [nt(modes, pick[pl.ds(128 * j, 128), :]) for j in range(SLOTS)]
    flat2 = out2.reshape(CHIPS * 8, 128)
    flat_near = near2.reshape(CHIPS * 4, 128)
    for q in range(4):
        block = jnp.concatenate(
            [y[8 * q : 8 * q + 8] for y in chosen] + [jnp.zeros((32, 128), f32)], axis=0
        )
        block = block.T
        flat_near[pl.ds(q, CHIPS, stride=4), :] = block[CHIPS:]
        flat2[pl.ds(core * 4 + q, CHIPS, stride=8), :] = block[:CHIPS]
    send(near2, out2.at[:, core], 5, sibling)
    settle(near2, 5)
    exchange(out2, in2, 1)

    for j in range(SLOTS):
        pltpu.make_async_copy(leg_ref.at[j], leg.at[j], leg_sem.at[j]).wait()
    degree = iota((16, DEGREES), 1).astype(f32)
    gain = jnp.where(degree > 0.5, -20000.0 / jnp.maximum(degree * (degree + 1.0), 1.0), 0.0)
    gain = jnp.where(iota((16, DEGREES), 0) // 4 % 2 == 1, gain, 1.0)
    row = iota((192, 128), 0)
    doubled = as_one_hot(iota((192, 128), 1) == row // 16 * 8 + row // 8 % 2 * 4 + row % 4)

    settle(in2, 1)
    mode_rows = nt(doubled, in2[...].reshape(CYCLES, 128).astype(bf16)).astype(bf16)
    for j in range(SLOTS):
        filt[j] = (nt(mode_rows[16 * j : 16 * j + 16], leg[j]) * gain).astype(bf16)
    for j in range(SLOTS):
        syn[pl.ds(16 * j, 16), :] = nn(filt[j], leg[j]).astype(bf16)

    col = iota((512, 512), 1)
    device = 2 * (col & 63) + jnp.where((col & 127) < CHIPS, core, 1 - core)
    by_quad = as_one_hot(iota((512, 512), 0) == device * 4 + (col >> 7))
    maps = nn(syn[...], by_quad)
    for h in range(6):
        block = jnp.concatenate(
            [
                maps[16 * j : 16 * j + 16, 128 * q : 128 * q + 128]
                for j in (2 * h, 2 * h + 1)
                for q in range(4)
            ],
            axis=0,
        ).T
        near3[pl.ds(CHIPS * h, CHIPS), :] = block[CHIPS:].astype(bf16)
        stage[pl.ds(core * 8 + h, CHIPS, stride=16), :] = block[:CHIPS]
    send(near3, got3, 6, sibling)
    settle(near3, 6)
    for h in range(6):
        piece = got3[pl.ds(CHIPS * h, CHIPS), :].astype(f32)
        stage[pl.ds(8 - core * 8 + h, CHIPS, stride=16), :] = piece
    out3[...] = stage[...].astype(bf16).reshape(CHIPS, 16, 128)
    exchange(out3, in3, 2)
    settle(in3, 2)

    stage[...] = in3[...].reshape(CHIPS * 16, 128).astype(f32)
    lefts = []
    for h in range(6):
        block = jnp.concatenate(
            [
                stage[pl.ds(core * 8 + h, CHIPS, stride=16), :],
                stage[pl.ds(8 - core * 8 + h, CHIPS, stride=16), :],
            ],
            axis=0,
        ).T.astype(bf16)
        lefts += [block[:64], block[64:]]
    v = nn(jnp.concatenate(lefts, axis=1), pick[...])
    v = (v * jnp.where(iota((1, 2048), 1) == 0, 1.0, 2.0)).astype(bf16)
    rights = [None] * 4
    for odd in range(2):
        left = jnp.concatenate(
            [
                v[16 * q : 16 * q + 16, 128 * h : 128 * h + 128]
                for h in range(16)
                for q in (odd, odd + 2)
            ],
            axis=0,
        )
        g = nn(jnp.concatenate([left, left], axis=1), back[odd])
        g = g.reshape(16, 2, 2, 8, 512)
        parts = ([], [])
        for par in range(2):
            at = 256 * par
            g0c, g0s = g[:, :, 0, :, at : at + 128], g[:, :, 0, :, at + 128 : at + 256]
            g1c, g1s = g[:, :, 1, :, at : at + 128], g[:, :, 1, :, at + 128 : at + 256]
            ur, ui = g0c - g1s, g0s + g1c
            tc, ts = unwind[odd, 0, par][:, None], unwind[odd, 1, par][:, None]
            er, ei = ur * tc - ui * ts, ur * ts + ui * tc
            for k in range(2):
                parts[k].append(er[:, k].reshape(128, 128))
                parts[k].append(ei[:, k].reshape(128, 128))
        for k in range(2):
            rights[odd + 2 * k] = jnp.concatenate(parts[k], axis=0)
    for k in range(2):
        high, low = two_parts(jnp.concatenate(rights[2 * k : 2 * k + 2], axis=1))
        sky = nn(last_h[...], high) + nn(last_h[...], low) + nn(last_l[...], high)
        for q in range(2):
            one = sky[:, 128 * q : 128 * q + 128].reshape(2, 4, 32, 128)
            for b in range(NBIN):
                kappa_ref[b, pl.ds(2 * k + q, 32, stride=4), :] = one[0, b]
                potential_ref[b, pl.ds(2 * k + q, 32, stride=4), :] = one[1, b]

    sent(id1.at[pl.ds(0, LOCAL - 1)], 3)
    sent(id2.at[pl.ds(0, BANDS - 1)], 4)
    sent(in1.at[pl.ds(0, DEVICES - 1)], 0)
    sent(near2, 5)
    sent(near3, 6)
    sent(in2.at[pl.ds(0, CHIPS - 1)], 1)
    sent(in3.at[pl.ds(0, CHIPS - 1)], 2)


def per_device(weights, offsets, counts, block_ids, m_table, legendre):
    constants = [jnp.asarray(t) for t in tables()]
    vmem = pl.BlockSpec(memory_space=pltpu.VMEM)
    hbm = pl.BlockSpec(memory_space=pltpu.HBM)
    shape = jax.ShapeDtypeStruct((NBIN, 128, 128), f32)
    kappa, potential = pl.pallas_call(
        kernel,
        out_shape=(pltpu.VMEM(shape.shape, f32),) * 2,
        in_specs=[vmem] * 5 + [hbm] * 11,
        out_specs=(vmem, vmem),
        scratch_shapes=[
            *[pltpu.VMEM(t.shape, t.dtype) for t in constants],
            pltpu.VMEM((SLOTS, DEGREES, CYCLES), bf16),
            pltpu.VMEM((DEVICES, 32, 128), bf16),
            pltpu.VMEM((DEVICES, 32, 128), bf16),
            pltpu.VMEM((CHIPS, 4, 128), f32),
            pltpu.VMEM((CHIPS, 2, 4, 128), f32),
            pltpu.VMEM((CHIPS, 2, 4, 128), f32),
            pltpu.VMEM((CHIPS * 6, 128), bf16),
            pltpu.VMEM((CHIPS * 6, 128), bf16),
            pltpu.VMEM((CHIPS, 16, 128), bf16),
            pltpu.VMEM((CHIPS, 16, 128), bf16),
            pltpu.VMEM((CHIPS * 16, 128), f32),
            pltpu.VMEM((CAP, DEVICES), f32),
            pltpu.VMEM((LOCAL, CAP, DEVICES), f32),
            pltpu.VMEM((BANDS, 1, 128), f32),
            pltpu.VMEM((BANDS, 1, 128), f32),
            pltpu.VMEM((512, 4096), bf16),
            pltpu.VMEM((SLOTS * 128, 2048), bf16),
            pltpu.VMEM((SLOTS, 16, DEGREES), bf16),
            pltpu.VMEM((SLOTS * 16, CYCLES), bf16),
            pltpu.SemaphoreType.DMA((10,)),
            pltpu.SemaphoreType.DMA((SLOTS,)),
            pltpu.SemaphoreType.DMA((7,)),
            pltpu.SemaphoreType.DMA((7,)),
            pltpu.SemaphoreType.DMA((4,)),
        ],
        compiler_params=pltpu.CompilerParams(
            collective_id=0, has_side_effects=True, vmem_limit_bytes=60 << 20
        ),
        name="deposit_filter",
    )(
        weights[0].reshape(DEVICES, CAP * NBIN, 128),
        offsets[0],
        jnp.swapaxes(block_ids, 1, 2).reshape(CAP, DEVICES),
        counts,
        m_table,
        legendre,
        *constants,
    )
    maps = [x.reshape(NBIN, 32, 4, 128).transpose(0, 2, 1, 3) for x in (kappa, potential)]
    return tuple(x.reshape(NBIN, 4, NPHI) for x in maps)


def solution(mesh):
    placed = (
        P(("blk", "ma"), None, None, None, None),
        P(("blk", "ma"), None, None, None),
        P(("blk", "ma"), None),
        P(("blk", "ma"), None, None),
        P(),
        P(("blk", "ma"), None, None),
    )
    return jax.shard_map(
        per_device,
        mesh=mesh,
        in_specs=placed,
        out_specs=(P(None, ("blk", "ma"), None), P(None, ("blk", "ma"), None)),
        check_vma=False,
    )
```

```python
import math

import jax
import jax.numpy as jnp
import numpy as np
from jax import lax
from jax.experimental import pallas as pl
from jax.experimental.pallas import tpu as pltpu
from jax.sharding import PartitionSpec as P

NPHI = 4096
BANDS = 16
LOCAL = 8
DEVICES = BANDS * LOCAL
CHIPS = DEVICES // 2
CAP = 8
NBIN = 4
SLOTS = 12
DEGREES = 1664
CYCLES = 512
PART = 32
BATCH = 8
STRIDE = 27
EARLY = 24
MESH_IDS = pl.DeviceIdType.MESH
bf16 = jnp.bfloat16
f32 = jnp.float32


def nn(a, b):
    return lax.dot_general(a, b, (((1,), (0,)), ((), ())), preferred_element_type=f32)


def nt(a, b):
    return lax.dot_general(a, b, (((1,), (1,)), ((), ())), preferred_element_type=f32)


def two_parts(x):
    high = x.astype(bf16)
    return high, (x - high.astype(f32)).astype(bf16)


def iota(shape, axis):
    return lax.broadcasted_iota(jnp.int32, shape, axis)


def as_one_hot(mask):
    return jnp.where(mask, 1.0, 0.0).astype(bf16)


def tables():
    import ml_dtypes

    def halves(x):
        high = x.astype(np.float32).astype(ml_dtypes.bfloat16)
        low = (x - high.astype(np.float64)).astype(np.float32).astype(ml_dtypes.bfloat16)
        return high, low

    turn = 2.0 * np.pi
    pair, par, quad = np.arange(16), np.arange(2), np.arange(4)
    kb, p, m2 = np.arange(32), np.arange(128), np.arange(64)
    m1 = 2 * pair[None, :] + par[:, None]
    keep = (m2 < 48).astype(np.float64)
    angle = turn * (m1[:, :, None] * kb % 32) / 32
    both = np.stack([np.cos(angle), -np.sin(angle)]) / NPHI
    first = np.einsum("rabk,qs->rabqsk", both, np.eye(4)).reshape(256, 128)
    shift = (quad % 2) / 2.0
    angle = turn * m1[:, :, None, None] * (p[None, :] + shift[:, None]) / NPHI
    twiddle = np.stack([np.cos(angle), np.sin(angle)]).reshape(2, 128, 128)
    angle = turn * (p[:, None] * m2[None, :] % 128) / 128
    c, s = np.cos(angle) * keep, np.sin(angle) * keep
    square = np.array([[c, -s], [s, c]])
    second = np.einsum("iopm,ab->aipobm", square, np.eye(2)).reshape(512, 256)
    angle = np.tile(np.pi * m2 / 128, 2)
    half = np.stack([np.cos(angle), np.sin(angle)])
    half = np.concatenate([half, np.zeros((6, 128))])
    back = []
    for odd in range(2):
        angle = turn * m2[:, None] * (p[None, :] + odd / 2.0) / 128
        value = np.stack([np.cos(angle), np.sin(angle)]) * keep[None, :, None]
        back.append(np.einsum("rmp,ab->ambrp", value, np.eye(2)).reshape(128, 512))
    back = np.stack(back)
    odd = np.arange(2) / 2.0
    angle = turn * m1[None, :, :, None] * (p + odd[:, None, None, None]) / NPHI
    unwind = np.stack([np.cos(angle), np.sin(angle)], axis=1).reshape(2, 2, 2, 16, 1, 128)
    angle = turn * (m1[:, :, None] * kb % 32) / 32
    both = np.stack([np.cos(angle), -np.sin(angle)], axis=1)
    last = np.einsum("aihk,uv->ukaihv", both, np.eye(8)).reshape(256, 512)
    back_parts = halves(back)
    return (
        *halves(first),
        twiddle.astype(np.float32),
        *halves(second),
        half.astype(np.float32),
        np.concatenate(back_parts, axis=1),
        unwind.astype(np.float32),
        *halves(last),
    )


def place(index):
    return (index // LOCAL, lax.rem(index, LOCAL))


def kernel(*refs):
    (
        w_hbm, off_hbm, blocks_ref, counts_ref, orders_ref, leg_ref, *constants,
    ) = refs[:16]
    kappa_ref, potential_ref = refs[16:18]
    held = refs[18:28]
    first_h, first_l, twiddle, second_h, second_l, half, back, unwind, last_h, last_l = held
    (
        leg, out1, in1, near2, out2, in2, near3, got3, out3, in3, stage, id0, id1, idx, id2, sel, pick, filt, syn,
        w_ref, off_ref, order, doubled, by_quad, gain, load_sem, const_sem, leg_sem, send_sem, recv_sem, part_sem,
    ) = refs[28:]
    band = lax.axis_index("blk")
    local = lax.axis_index("ma")
    me = band * LOCAL + local
    core = lax.rem(local, 2)
    chip = me // 2
    sibling = (band, local + 1 - 2 * core)

    loads = []
    for k in range(4):
        rows = pl.ds(32 * k, 32)
        loads.append(pltpu.make_async_copy(w_hbm.at[rows], w_ref.at[rows], load_sem.at[2 * k]))
        loads.append(
            pltpu.make_async_copy(off_hbm.at[rows], off_ref.at[rows], load_sem.at[2 * k + 1])
        )
    for load in loads:
        load.start()

    barrier = pltpu.get_barrier_semaphore()

    def greet(i, carry):
        pl.semaphore_signal(
            barrier, inc=1, device_id=place(lax.rem(me + i, DEVICES)), device_id_type=MESH_IDS
        )
        return carry

    lax.fori_loop(1, DEVICES, greet, 0)

    def send(src, dst, k, target):
        pltpu.make_async_remote_copy(
            src_ref=src,
            dst_ref=dst,
            send_sem=send_sem.at[k],
            recv_sem=recv_sem.at[k],
            device_id=target,
            device_id_type=MESH_IDS,
        ).start()

    def settle(ref, k):
        pltpu.make_async_copy(ref, ref, recv_sem.at[k]).wait()

    def sent(ref, k):
        pltpu.make_async_copy(ref, ref, send_sem.at[k]).wait()

    def exchange(out, into, k):
        pltpu.make_async_copy(out.at[chip], into.at[chip], recv_sem.at[k]).start()

        def one(i, carry):
            t = lax.rem(chip + i, CHIPS)
            send(out.at[t], into.at[chip], k, place(2 * t + core))
            return carry

        lax.fori_loop(1, CHIPS, one, 0)

    for n in range(10):
        pltpu.make_async_copy(constants[n], held[n], const_sem.at[n]).start()
    for j in range(SLOTS):
        pltpu.make_async_copy(leg_ref.at[j], leg.at[j], leg_sem.at[j]).start()

    pixel = iota((128, 128), 0).astype(f32).astype(bf16)
    group_of_row = iota((32, 128), 0) // 4

    def target(i):
        step = lax.rem(i * STRIDE, DEVICES)
        return lax.rem(band + step // LOCAL, BANDS), lax.rem(local + lax.rem(step, LOCAL), LOCAL)

    def deposit(i, carry):
        t = target(i)
        t = t[0] * LOCAL + t[1]
        w = w_ref[t]
        offs = off_ref[t].astype(f32).astype(bf16)
        left = jnp.concatenate(
            [jnp.where(group_of_row == c, w, jnp.zeros_like(w)) for c in range(CAP)], axis=1
        )
        one, zero = jnp.ones((), bf16), jnp.zeros((), bf16)
        right = jnp.concatenate(
            [jnp.where(offs[c : c + 1, :] == pixel, one, zero) for c in range(CAP)], axis=1
        )
        out1[i] = nt(left, right).astype(bf16)
        return carry

    def send_part(i, k):
        pltpu.make_async_remote_copy(
            src_ref=out1.at[i],
            dst_ref=in1.at[i],
            send_sem=send_sem.at[0],
            recv_sem=part_sem.at[k],
            device_id=target(i),
            device_id_type=MESH_IDS,
        ).start()

    live = iota((CAP, DEVICES), 0) < counts_ref[...]
    id0[...] = jnp.where(live, blocks_ref[...], -1).astype(f32)
    for load in loads:
        load.wait()
    lax.fori_loop(0, EARLY, deposit, 0, unroll=4)
    pl.semaphore_wait(barrier, DEVICES - 1)

    pltpu.make_async_copy(id0, id1.at[local], recv_sem.at[3]).start()
    for i in range(1, LOCAL):
        send(id0, id1.at[local], 3, (band, lax.rem(local + i, LOCAL)))

    pltpu.make_async_copy(out1.at[0], in1.at[0], part_sem.at[0]).start()

    def early(i, carry):
        send_part(i, 0)
        return carry

    lax.fori_loop(1, EARLY, early, 0)

    def deposit_send(k):
        def step(n, carry):
            for u in range(BATCH):
                deposit(n * BATCH + u, carry)
            for u in range(BATCH):
                send_part(n * BATCH + u, k)
            return carry

        return step

    lax.fori_loop(EARLY // BATCH, PART // BATCH, deposit_send(0), 0)
    lax.fori_loop(1 * PART // BATCH, 2 * PART // BATCH, deposit_send(1), 0)

    settle(id1, 3)
    column = as_one_hot(iota((BANDS, DEVICES), 1) == iota((BANDS, DEVICES), 0) * LOCAL + local)
    every = id1[...].reshape(LOCAL * CAP, DEVICES).astype(bf16)
    every = nt(column, jnp.concatenate([every, every], axis=0))
    for i in range(BANDS):
        idx[i] = every[i : i + 1]
    pltpu.make_async_copy(idx.at[band], id2.at[band], recv_sem.at[4]).start()
    for i in range(1, BANDS):
        t = lax.rem(band + i, BANDS)
        send(idx.at[t], id2.at[band], 4, (t, local))

    lax.fori_loop(2 * PART // BATCH, 3 * PART // BATCH, deposit_send(2), 0)
    lax.fori_loop(3 * PART // BATCH, 4 * PART // BATCH, deposit_send(3), 0)

    slot = iota((DEVICES, 1536), 1)
    owner = (slot * 5462) >> 16
    orders = jnp.broadcast_to(orders_ref[...].reshape(1, 1536), (DEVICES, 1536)).astype(f32)
    row = iota((DEVICES, 1536), 0)
    device = 2 * (row & 63) + jnp.where(row < CHIPS, core, 1 - core)
    orders = jnp.where(owner == device, orders, 0.0)
    slot = iota((16, 1536), 1)
    which = as_one_hot(slot - ((slot * 5462) >> 16) * SLOTS == iota((16, 1536), 0))
    high, low = two_parts(orders)
    orders = nt(high, which) + nt(low, which)

    stage[...] = jnp.zeros_like(stage)

    lane = iota((1, 2048), 1)
    m2 = lane % 64
    label = jnp.where(m2 < 48, lane // 128 * 2 + lane // 64 % 2 + 32 * m2, -1).astype(f32)
    for j in range(SLOTS):
        pick[pl.ds(128 * j, 128), :] = as_one_hot(orders[:, j : j + 1] == label)

    row = iota((512, 1), 0)
    origin = ((row >> 2) & 1) * 256 + (row & 3) * 64 + (row >> 5) * 4 + ((row >> 3) & 3)
    order[...] = as_one_hot(iota((512, 512), 1) == origin)
    row = iota((192, 1), 0)
    origin = (row >> 4) * 8 + ((row >> 3) & 1) * 4 + (row & 3)
    doubled[...] = as_one_hot(iota((192, 128), 1) == origin)
    col = iota((1, 512), 1)
    device = 2 * (col & 63) + jnp.where((col & 127) < CHIPS, core, 1 - core)
    by_quad[...] = as_one_hot(iota((512, 512), 0) == device * 4 + (col >> 7))
    degree = iota((16, DEGREES), 1).astype(f32)
    filter_gain = jnp.where(
        degree > 0.5, -20000.0 / jnp.maximum(degree * (degree + 1.0), 1.0), 0.0
    )
    gain[...] = jnp.where(((iota((16, DEGREES), 0) >> 2) & 1) == 1, filter_gain, 1.0)

    settle(id2, 4)
    at = iota((128, 4096), 1)
    step = (at >> 5) * STRIDE & 127
    wide = as_one_hot(iota((128, 4096), 0) == (local - step & 7) * CAP + ((at >> 2) & 7))
    spread = nn(id2[...].reshape(BANDS, 128).astype(bf16), wide)
    at = iota((BANDS, 4096), 1)
    step = (at >> 5) * STRIDE & 127
    spread = jnp.where((band - (step >> 3) & 15) == iota((BANDS, 4096), 0), spread, 0.0)
    ids_row = jnp.sum(spread, axis=0, keepdims=True)
    bin_row = (iota((1, 4096), 1) & 3).astype(f32)
    ids_row = jnp.where(ids_row < 0.0, -1.0, ids_row + 128.0 * bin_row)
    for b in range(NBIN):
        rows = (iota((128, 4096), 0) + 128 * b).astype(f32)
        sel[pl.ds(128 * b, 128), :] = as_one_hot(ids_row == rows)

    for n in range(10):
        pltpu.make_async_copy(constants[n], held[n], const_sem.at[n]).wait()
    counted = None
    for k in range(4):
        piece = in1.at[pl.ds(PART * k, PART)]
        pltpu.make_async_copy(piece, piece, part_sem.at[k]).wait()
        term = nn(sel[:, 1024 * k : 1024 * k + 1024], piece[...].reshape(1024, 128))
        counted = term if counted is None else counted + term

    lefts = []
    high, low = two_parts(
        jnp.concatenate([counted[128 * b : 128 * b + 128] for b in range(NBIN)], axis=1)
    )
    both = jnp.concatenate([first_h[...], first_l[...]], axis=1)
    every = nn(both, jnp.concatenate([high, high], axis=0)) + nn(first_h[...], low)
    for b in range(NBIN):
        z = every[:, 128 * b : 128 * b + 128]
        zr, zi = z[:128], z[128:]
        ar = zr * twiddle[0] + zi * twiddle[1]
        ai = zi * twiddle[0] - zr * twiddle[1]
        lefts.append(jnp.concatenate([ar[:64], ai[:64], ar[64:], ai[64:]], axis=1))
    high, low = two_parts(jnp.concatenate(lefts, axis=0))
    x = nn(high, second_h[...]) + nn(low, second_h[...]) + nn(high, second_l[...])
    xr, xi = x[:, :128], x[:, 128:]
    odd = iota((256, 128), 0) % 2 == 1
    c = jnp.where(odd, half[0:1, :], 1.0)
    s = jnp.where(odd, half[1:2, :], 0.0)
    modes = jnp.concatenate([xr * c + xi * s, xi * c - xr * s], axis=0).astype(bf16)
    modes = nn(order[...], modes).astype(bf16)
    modes = jnp.concatenate([modes[32 * h : 32 * h + 32] for h in range(16)], axis=1)
    chosen = [nt(modes, pick[pl.ds(128 * j, 128), :]) for j in range(SLOTS)]
    flat2 = out2.reshape(CHIPS * 8, 128)
    flat_near = near2.reshape(CHIPS * 4, 128)
    for q in range(4):
        block = jnp.concatenate(
            [y[8 * q : 8 * q + 8] for y in chosen] + [jnp.zeros((32, 128), f32)], axis=0
        )
        block = block.T
        flat_near[pl.ds(q, CHIPS, stride=4), :] = block[CHIPS:]
        flat2[pl.ds(core * 4 + q, CHIPS, stride=8), :] = block[:CHIPS]
    send(near2, out2.at[:, core], 5, sibling)
    settle(near2, 5)
    exchange(out2, in2, 1)

    for j in range(SLOTS):
        pltpu.make_async_copy(leg_ref.at[j], leg.at[j], leg_sem.at[j]).wait()
    settle(in2, 1)
    mode_rows = nt(doubled[...], in2[...].reshape(CYCLES, 128).astype(bf16)).astype(bf16)
    for j in range(SLOTS + 1):
        if j < SLOTS:
            filt[j] = (nt(mode_rows[16 * j : 16 * j + 16], leg[j]) * gain[...]).astype(bf16)
        if j > 0:
            syn[pl.ds(16 * j - 16, 16), :] = nn(filt[j - 1], leg[j - 1]).astype(bf16)

    maps = nn(syn[...], by_quad[...])
    for h in range(6):
        block = jnp.concatenate(
            [
                maps[16 * j : 16 * j + 16, 128 * q : 128 * q + 128]
                for j in (2 * h, 2 * h + 1)
                for q in range(4)
            ],
            axis=0,
        ).T
        near3[pl.ds(CHIPS * h, CHIPS), :] = block[CHIPS:].astype(bf16)
        stage[pl.ds(core * 8 + h, CHIPS, stride=16), :] = block[:CHIPS]
    send(near3, got3, 6, sibling)
    settle(near3, 6)
    for h in range(6):
        piece = got3[pl.ds(CHIPS * h, CHIPS), :].astype(f32)
        stage[pl.ds(8 - core * 8 + h, CHIPS, stride=16), :] = piece
    out3[...] = stage[...].astype(bf16).reshape(CHIPS, 16, 128)
    exchange(out3, in3, 2)
    settle(in3, 2)

    stage[...] = in3[...].reshape(CHIPS * 16, 128).astype(f32)
    lefts = []
    for h in range(6):
        block = jnp.concatenate(
            [
                stage[pl.ds(core * 8 + h, CHIPS, stride=16), :],
                stage[pl.ds(8 - core * 8 + h, CHIPS, stride=16), :],
            ],
            axis=0,
        ).T.astype(bf16)
        lefts += [block[:64], block[64:]]
    v = nn(jnp.concatenate(lefts, axis=1), pick[...])
    v = (v * jnp.where(iota((1, 2048), 1) == 0, 1.0, 2.0)).astype(bf16)
    rights = [None] * 4
    for odd in range(2):
        left = jnp.concatenate(
            [
                v[16 * q : 16 * q + 16, 128 * h : 128 * h + 128]
                for h in range(16)
                for q in (odd, odd + 2)
            ],
            axis=0,
        )
        g = nn(jnp.concatenate([left, left], axis=1), back[odd])
        g = g.reshape(16, 2, 2, 8, 512)
        parts = ([], [])
        for par in range(2):
            at = 256 * par
            g0c, g0s = g[:, :, 0, :, at : at + 128], g[:, :, 0, :, at + 128 : at + 256]
            g1c, g1s = g[:, :, 1, :, at : at + 128], g[:, :, 1, :, at + 128 : at + 256]
            ur, ui = g0c - g1s, g0s + g1c
            tc, ts = unwind[odd, 0, par][:, None], unwind[odd, 1, par][:, None]
            er, ei = ur * tc - ui * ts, ur * ts + ui * tc
            for k in range(2):
                parts[k].append(er[:, k].reshape(128, 128))
                parts[k].append(ei[:, k].reshape(128, 128))
        for k in range(2):
            rights[odd + 2 * k] = jnp.concatenate(parts[k], axis=0)
    for k in range(2):
        high, low = two_parts(jnp.concatenate(rights[2 * k : 2 * k + 2], axis=1))
        sky = nn(last_h[...], high) + nn(last_h[...], low) + nn(last_l[...], high)
        for q in range(2):
            one = sky[:, 128 * q : 128 * q + 128].reshape(2, 4, 32, 128)
            for b in range(NBIN):
                kappa_ref[b, pl.ds(2 * k + q, 32, stride=4), :] = one[0, b]
                potential_ref[b, pl.ds(2 * k + q, 32, stride=4), :] = one[1, b]

    sent(id1.at[pl.ds(0, LOCAL - 1)], 3)
    sent(id2.at[pl.ds(0, BANDS - 1)], 4)
    sent(in1.at[pl.ds(0, DEVICES - 1)], 0)
    sent(near2, 5)
    sent(near3, 6)
    sent(in2.at[pl.ds(0, CHIPS - 1)], 1)
    sent(in3.at[pl.ds(0, CHIPS - 1)], 2)


def per_device(weights, offsets, counts, block_ids, m_table, legendre):
    constants = [jnp.asarray(t) for t in tables()]
    vmem = pl.BlockSpec(memory_space=pltpu.VMEM)
    hbm = pl.BlockSpec(memory_space=pltpu.HBM)
    shape = jax.ShapeDtypeStruct((NBIN, 128, 128), f32)
    kappa, potential = pl.pallas_call(
        kernel,
        out_shape=(pltpu.VMEM(shape.shape, f32),) * 2,
        in_specs=[hbm] * 2 + [vmem] * 3 + [hbm] * 11,
        out_specs=(vmem, vmem),
        scratch_shapes=[
            *[pltpu.VMEM(t.shape, t.dtype) for t in constants],
            pltpu.VMEM((SLOTS, DEGREES, CYCLES), bf16),
            pltpu.VMEM((DEVICES, 32, 128), bf16),
            pltpu.VMEM((DEVICES, 32, 128), bf16),
            pltpu.VMEM((CHIPS, 4, 128), f32),
            pltpu.VMEM((CHIPS, 2, 4, 128), f32),
            pltpu.VMEM((CHIPS, 2, 4, 128), f32),
            pltpu.VMEM((CHIPS * 6, 128), bf16),
            pltpu.VMEM((CHIPS * 6, 128), bf16),
            pltpu.VMEM((CHIPS, 16, 128), bf16),
            pltpu.VMEM((CHIPS, 16, 128), bf16),
            pltpu.VMEM((CHIPS * 16, 128), f32),
            pltpu.VMEM((CAP, DEVICES), f32),
            pltpu.VMEM((LOCAL, CAP, DEVICES), f32),
            pltpu.VMEM((BANDS, 1, 128), f32),
            pltpu.VMEM((BANDS, 1, 128), f32),
            pltpu.VMEM((512, 4096), bf16),
            pltpu.VMEM((SLOTS * 128, 2048), bf16),
            pltpu.VMEM((SLOTS, 16, DEGREES), bf16),
            pltpu.VMEM((SLOTS * 16, CYCLES), bf16),
            pltpu.VMEM((DEVICES, CAP * NBIN, 128), bf16),
            pltpu.VMEM((DEVICES, CAP, 128), jnp.int32),
            pltpu.VMEM((512, 512), bf16),
            pltpu.VMEM((SLOTS * 16, 128), bf16),
            pltpu.VMEM((512, 512), bf16),
            pltpu.VMEM((16, DEGREES), f32),
            pltpu.SemaphoreType.DMA((8,)),
            pltpu.SemaphoreType.DMA((10,)),
            pltpu.SemaphoreType.DMA((SLOTS,)),
            pltpu.SemaphoreType.DMA((7,)),
            pltpu.SemaphoreType.DMA((7,)),
            pltpu.SemaphoreType.DMA((4,)),
        ],
        compiler_params=pltpu.CompilerParams(
            collective_id=0, has_side_effects=True, vmem_limit_bytes=60 << 20
        ),
        name="deposit_filter",
    )(
        weights[0].reshape(DEVICES, CAP * NBIN, 128),
        offsets[0],
        jnp.swapaxes(block_ids, 1, 2).reshape(CAP, DEVICES),
        counts,
        m_table,
        legendre,
        *constants,
    )
    maps = [x.reshape(NBIN, 32, 4, 128).transpose(0, 2, 1, 3) for x in (kappa, potential)]
    return tuple(x.reshape(NBIN, 4, NPHI) for x in maps)


def solution(mesh):
    placed = (
        P(("blk", "ma"), None, None, None, None),
        P(("blk", "ma"), None, None, None),
        P(("blk", "ma"), None),
        P(("blk", "ma"), None, None),
        P(),
        P(("blk", "ma"), None, None),
    )
    return jax.shard_map(
        per_device,
        mesh=mesh,
        in_specs=placed,
        out_specs=(P(None, ("blk", "ma"), None), P(None, ("blk", "ma"), None)),
        check_vma=False,
    )
```

```python
import math

import jax
import jax.numpy as jnp
import numpy as np
from jax import lax
from jax.experimental import pallas as pl
from jax.experimental.pallas import tpu as pltpu
from jax.sharding import PartitionSpec as P

NPHI = 4096
BANDS = 16
LOCAL = 8
DEVICES = BANDS * LOCAL
CHIPS = DEVICES // 2
CAP = 8
NBIN = 4
SLOTS = 12
DEGREES = 1664
CYCLES = 512
PART = 32
BATCH = 8
STRIDE = 27
EARLY = 24
MESH_IDS = pl.DeviceIdType.MESH
bf16 = jnp.bfloat16
f32 = jnp.float32


def nn(a, b):
    return lax.dot_general(a, b, (((1,), (0,)), ((), ())), preferred_element_type=f32)


def nt(a, b):
    return lax.dot_general(a, b, (((1,), (1,)), ((), ())), preferred_element_type=f32)


def two_parts(x):
    high = x.astype(bf16)
    return high, (x - high.astype(f32)).astype(bf16)


def iota(shape, axis):
    return lax.broadcasted_iota(jnp.int32, shape, axis)


def as_one_hot(mask):
    return jnp.where(mask, 1.0, 0.0).astype(bf16)


def tables():
    import ml_dtypes

    def halves(x):
        high = x.astype(np.float32).astype(ml_dtypes.bfloat16)
        low = (x - high.astype(np.float64)).astype(np.float32).astype(ml_dtypes.bfloat16)
        return high, low

    turn = 2.0 * np.pi
    pair, par, quad = np.arange(16), np.arange(2), np.arange(4)
    kb, p, m2 = np.arange(32), np.arange(128), np.arange(64)
    m1 = 2 * pair[None, :] + par[:, None]
    keep = (m2 < 48).astype(np.float64)
    angle = turn * (m1[:, :, None] * kb % 32) / 32
    both = np.stack([np.cos(angle), -np.sin(angle)]) / NPHI
    first = np.einsum("rabk,qs->rabqsk", both, np.eye(4)).reshape(256, 128)
    shift = (quad % 2) / 2.0
    angle = turn * m1[:, :, None, None] * (p[None, :] + shift[:, None]) / NPHI
    twiddle = np.stack([np.cos(angle), np.sin(angle)]).reshape(2, 128, 128)
    angle = turn * (p[:, None] * m2[None, :] % 128) / 128
    c, s = np.cos(angle) * keep, np.sin(angle) * keep
    square = np.array([[c, -s], [s, c]])
    second = np.einsum("iopm,ab->aipobm", square, np.eye(2)).reshape(512, 256)
    angle = np.tile(np.pi * m2 / 128, 2)
    half = np.stack([np.cos(angle), np.sin(angle)])
    half = np.concatenate([half, np.zeros((6, 128))])
    back = []
    for odd in range(2):
        angle = turn * m2[:, None] * (p[None, :] + odd / 2.0) / 128
        value = np.stack([np.cos(angle), np.sin(angle)]) * keep[None, :, None]
        back.append(np.einsum("rmp,ab->ambrp", value, np.eye(2)).reshape(128, 512))
    back = np.stack(back)
    odd = np.arange(2) / 2.0
    angle = turn * m1[None, :, :, None] * (p + odd[:, None, None, None]) / NPHI
    unwind = np.stack([np.cos(angle), np.sin(angle)], axis=1).reshape(2, 2, 2, 16, 1, 128)
    angle = turn * (m1[:, :, None] * kb % 32) / 32
    both = np.stack([np.cos(angle), -np.sin(angle)], axis=1)
    last = np.einsum("aihk,uv->ukaihv", both, np.eye(8)).reshape(256, 512)
    back_parts = halves(back)
    return (
        *halves(first),
        twiddle.astype(np.float32),
        *halves(second),
        half.astype(np.float32),
        np.concatenate(back_parts, axis=1),
        unwind.astype(np.float32),
        *halves(last),
    )


def place(index):
    return (index // LOCAL, lax.rem(index, LOCAL))


def kernel(*refs):
    (
        w_hbm, off_hbm, blocks_ref, counts_ref, orders_ref, leg_ref, *constants,
    ) = refs[:16]
    kappa_ref, potential_ref = refs[16:18]
    held = refs[18:28]
    first_h, first_l, twiddle, second_h, second_l, half, back, unwind, last_h, last_l = held
    (
        leg, out1, in1, near2, out2, in2, near3, got3, out3, in3, stage, id0, id1, idx, id2, sel, pick, filt, syn,
        w_ref, off_ref, order, doubled, by_quad, gain, load_sem, const_sem, leg_sem, send_sem, recv_sem, part_sem,
    ) = refs[28:]
    band = lax.axis_index("blk")
    local = lax.axis_index("ma")
    me = band * LOCAL + local
    core = lax.rem(local, 2)
    chip = me // 2
    sibling = (band, local + 1 - 2 * core)

    loads = []
    for k in range(4):
        rows = pl.ds(32 * k, 32)
        loads.append(pltpu.make_async_copy(w_hbm.at[rows], w_ref.at[rows], load_sem.at[2 * k]))
        loads.append(
            pltpu.make_async_copy(off_hbm.at[rows], off_ref.at[rows], load_sem.at[2 * k + 1])
        )
    for load in loads:
        load.start()

    barrier = pltpu.get_barrier_semaphore()

    def greet(i, carry):
        pl.semaphore_signal(
            barrier, inc=1, device_id=place(lax.rem(me + i, DEVICES)), device_id_type=MESH_IDS
        )
        return carry

    lax.fori_loop(1, DEVICES, greet, 0)

    def send(src, dst, k, target):
        pltpu.make_async_remote_copy(
            src_ref=src,
            dst_ref=dst,
            send_sem=send_sem.at[k],
            recv_sem=recv_sem.at[k],
            device_id=target,
            device_id_type=MESH_IDS,
        ).start()

    def settle(ref, k):
        pltpu.make_async_copy(ref, ref, recv_sem.at[k]).wait()

    def sent(ref, k):
        pltpu.make_async_copy(ref, ref, send_sem.at[k]).wait()

    def exchange(out, into, k):
        pltpu.make_async_copy(out.at[chip], into.at[chip], recv_sem.at[k]).start()

        def one(i, carry):
            t = lax.rem(chip + i, CHIPS)
            send(out.at[t], into.at[chip], k, place(2 * t + core))
            return carry

        lax.fori_loop(1, CHIPS, one, 0)

    for n in range(10):
        pltpu.make_async_copy(constants[n], held[n], const_sem.at[n]).start()
    for j in range(SLOTS):
        pltpu.make_async_copy(leg_ref.at[j], leg.at[j], leg_sem.at[j]).start()

    pixel = iota((128, 128), 0).astype(f32).astype(bf16)
    group_of_row = iota((32, 128), 0) // 4

    def target(i):
        step = lax.rem(i * STRIDE, DEVICES)
        return lax.rem(band + step // LOCAL, BANDS), lax.rem(local + lax.rem(step, LOCAL), LOCAL)

    def deposit(i, carry):
        t = target(i)
        t = t[0] * LOCAL + t[1]
        w = w_ref[t]
        offs = off_ref[t].astype(f32).astype(bf16)
        left = jnp.concatenate(
            [jnp.where(group_of_row == c, w, jnp.zeros_like(w)) for c in range(CAP)], axis=1
        )
        one, zero = jnp.ones((), bf16), jnp.zeros((), bf16)
        right = jnp.concatenate(
            [jnp.where(offs[c : c + 1, :] == pixel, one, zero) for c in range(CAP)], axis=1
        )
        out1[i] = nt(left, right).astype(bf16)
        return carry

    def send_part(i, k):
        pltpu.make_async_remote_copy(
            src_ref=out1.at[i],
            dst_ref=in1.at[i],
            send_sem=send_sem.at[0],
            recv_sem=part_sem.at[k],
            device_id=target(i),
            device_id_type=MESH_IDS,
        ).start()

    live = iota((CAP, DEVICES), 0) < counts_ref[...]
    id0[...] = jnp.where(live, blocks_ref[...], -1).astype(f32)
    for load in loads:
        load.wait()
    lax.fori_loop(0, EARLY, deposit, 0, unroll=4)
    pl.semaphore_wait(barrier, DEVICES - 1)

    pltpu.make_async_copy(id0, id1.at[local], recv_sem.at[3]).start()
    for i in range(1, LOCAL):
        send(id0, id1.at[local], 3, (band, lax.rem(local + i, LOCAL)))

    pltpu.make_async_copy(out1.at[0], in1.at[0], part_sem.at[0]).start()

    def early(i, carry):
        send_part(i, 0)
        return carry

    lax.fori_loop(1, EARLY, early, 0)

    def deposit_send(k):
        def step(n, carry):
            for u in range(BATCH):
                deposit(n * BATCH + u, carry)
            for u in range(BATCH):
                send_part(n * BATCH + u, k)
            return carry

        return step

    lax.fori_loop(EARLY // BATCH, PART // BATCH, deposit_send(0), 0)
    lax.fori_loop(1 * PART // BATCH, 2 * PART // BATCH, deposit_send(1), 0)

    settle(id1, 3)
    column = as_one_hot(iota((BANDS, DEVICES), 1) == iota((BANDS, DEVICES), 0) * LOCAL + local)
    every = id1[...].reshape(LOCAL * CAP, DEVICES).astype(bf16)
    every = nt(column, jnp.concatenate([every, every], axis=0))
    for i in range(BANDS):
        idx[i] = every[i : i + 1]
    pltpu.make_async_copy(idx.at[band], id2.at[band], recv_sem.at[4]).start()
    for i in range(1, BANDS):
        t = lax.rem(band + i, BANDS)
        send(idx.at[t], id2.at[band], 4, (t, local))

    lax.fori_loop(2 * PART // BATCH, 3 * PART // BATCH, deposit_send(2), 0)
    lax.fori_loop(3 * PART // BATCH, 4 * PART // BATCH, deposit_send(3), 0)

    slot = iota((DEVICES, 1536), 1)
    owner = (slot * 5462) >> 16
    orders = jnp.broadcast_to(orders_ref[...].reshape(1, 1536), (DEVICES, 1536)).astype(f32)
    row = iota((DEVICES, 1536), 0)
    device = 2 * (row & 63) + jnp.where(row < CHIPS, core, 1 - core)
    orders = jnp.where(owner == device, orders, 0.0)
    slot = iota((16, 1536), 1)
    which = as_one_hot(slot - ((slot * 5462) >> 16) * SLOTS == iota((16, 1536), 0))
    high, low = two_parts(orders)
    orders = nt(high, which) + nt(low, which)

    stage[...] = jnp.zeros_like(stage)

    lane = iota((1, 2048), 1)
    m2 = lane % 64
    label = jnp.where(m2 < 48, lane // 128 * 2 + lane // 64 % 2 + 32 * m2, -1).astype(f32)
    for j in range(SLOTS):
        pick[pl.ds(128 * j, 128), :] = as_one_hot(orders[:, j : j + 1] == label)

    row = iota((512, 1), 0)
    origin = ((row >> 2) & 1) * 256 + (row & 3) * 64 + (row >> 5) * 4 + ((row >> 3) & 3)
    order[...] = as_one_hot(iota((512, 512), 1) == origin)
    row = iota((192, 1), 0)
    origin = (row >> 4) * 8 + ((row >> 3) & 1) * 4 + (row & 3)
    doubled[...] = as_one_hot(iota((192, 128), 1) == origin)
    col = iota((1, 512), 1)
    device = 2 * (col & 63) + jnp.where((col & 127) < CHIPS, core, 1 - core)
    by_quad[...] = as_one_hot(iota((512, 512), 0) == device * 4 + (col >> 7))
    degree = iota((16, DEGREES), 1).astype(f32)
    filter_gain = jnp.where(
        degree > 0.5, -20000.0 / jnp.maximum(degree * (degree + 1.0), 1.0), 0.0
    )
    gain[...] = jnp.where(((iota((16, DEGREES), 0) >> 2) & 1) == 1, filter_gain, 1.0)

    settle(id2, 4)
    at = iota((128, 4096), 1)
    step = (at >> 5) * STRIDE & 127
    wide = as_one_hot(iota((128, 4096), 0) == (local - step & 7) * CAP + ((at >> 2) & 7))
    spread = nn(id2[...].reshape(BANDS, 128).astype(bf16), wide)
    at = iota((BANDS, 4096), 1)
    step = (at >> 5) * STRIDE & 127
    spread = jnp.where((band - (step >> 3) & 15) == iota((BANDS, 4096), 0), spread, 0.0)
    ids_row = jnp.sum(spread, axis=0, keepdims=True)
    bin_row = (iota((1, 4096), 1) & 3).astype(f32)
    ids_row = jnp.where(ids_row < 0.0, -1.0, ids_row + 128.0 * bin_row)
    for b in range(NBIN):
        rows = (iota((128, 4096), 0) + 128 * b).astype(f32)
        sel[pl.ds(128 * b, 128), :] = as_one_hot(ids_row == rows)

    for n in range(10):
        pltpu.make_async_copy(constants[n], held[n], const_sem.at[n]).wait()
    counted = None
    for k in range(4):
        piece = in1.at[pl.ds(PART * k, PART)]
        pltpu.make_async_copy(piece, piece, part_sem.at[k]).wait()
        term = nn(sel[:, 1024 * k : 1024 * k + 1024], piece[...].reshape(1024, 128))
        counted = term if counted is None else counted + term

    lefts = []
    high, low = two_parts(
        jnp.concatenate([counted[128 * b : 128 * b + 128] for b in range(NBIN)], axis=1)
    )
    both = jnp.concatenate([first_h[...], first_l[...]], axis=1)
    every = nn(both, jnp.concatenate([high, high], axis=0)) + nn(first_h[...], low)
    for b in range(NBIN):
        z = every[:, 128 * b : 128 * b + 128]
        zr, zi = z[:128], z[128:]
        ar = zr * twiddle[0] + zi * twiddle[1]
        ai = zi * twiddle[0] - zr * twiddle[1]
        lefts.append(jnp.concatenate([ar[:64], ai[:64], ar[64:], ai[64:]], axis=1))
    high, low = two_parts(jnp.concatenate(lefts, axis=0))
    x = nn(high, second_h[...]) + nn(low, second_h[...]) + nn(high, second_l[...])
    xr, xi = x[:, :128], x[:, 128:]
    odd = iota((256, 128), 0) % 2 == 1
    c = jnp.where(odd, half[0:1, :], 1.0)
    s = jnp.where(odd, half[1:2, :], 0.0)
    modes = jnp.concatenate([xr * c + xi * s, xi * c - xr * s], axis=0).astype(bf16)
    modes = nn(order[...], modes).astype(bf16)
    modes = jnp.concatenate([modes[32 * h : 32 * h + 32] for h in range(16)], axis=1)
    chosen = [nt(modes, pick[pl.ds(128 * j, 128), :]) for j in range(SLOTS)]
    flat2 = out2.reshape(CHIPS * 8, 128)
    flat_near = near2.reshape(CHIPS * 4, 128)
    own = []
    for q in range(4):
        block = jnp.concatenate(
            [y[8 * q : 8 * q + 8] for y in chosen] + [jnp.zeros((32, 128), f32)], axis=0
        )
        block = block.T
        flat_near[pl.ds(q, CHIPS, stride=4), :] = block[CHIPS:]
        own.append(block[:CHIPS])
    send(near2, out2.at[:, core], 5, sibling)
    for q in range(4):
        flat2[pl.ds(core * 4 + q, CHIPS, stride=8), :] = own[q]
    settle(near2, 5)
    exchange(out2, in2, 1)

    for j in range(SLOTS):
        pltpu.make_async_copy(leg_ref.at[j], leg.at[j], leg_sem.at[j]).wait()
    settle(in2, 1)
    mode_rows = nt(doubled[...], in2[...].reshape(CYCLES, 128).astype(bf16)).astype(bf16)
    for j in range(SLOTS + 1):
        if j < SLOTS:
            filt[j] = (nt(mode_rows[16 * j : 16 * j + 16], leg[j]) * gain[...]).astype(bf16)
        if j > 0:
            syn[pl.ds(16 * j - 16, 16), :] = nn(filt[j - 1], leg[j - 1]).astype(bf16)

    maps = nn(syn[...], by_quad[...])
    own = []
    for h in range(6):
        block = jnp.concatenate(
            [
                maps[16 * j : 16 * j + 16, 128 * q : 128 * q + 128]
                for j in (2 * h, 2 * h + 1)
                for q in range(4)
            ],
            axis=0,
        ).T
        near3[pl.ds(CHIPS * h, CHIPS), :] = block[CHIPS:].astype(bf16)
        own.append(block[:CHIPS])
    send(near3, got3, 6, sibling)
    for h in range(6):
        stage[pl.ds(core * 8 + h, CHIPS, stride=16), :] = own[h]
    settle(near3, 6)
    for h in range(6):
        piece = got3[pl.ds(CHIPS * h, CHIPS), :].astype(f32)
        stage[pl.ds(8 - core * 8 + h, CHIPS, stride=16), :] = piece
    out3[...] = stage[...].astype(bf16).reshape(CHIPS, 16, 128)
    exchange(out3, in3, 2)
    settle(in3, 2)

    stage[...] = in3[...].reshape(CHIPS * 16, 128).astype(f32)
    lefts = []
    for h in range(6):
        block = jnp.concatenate(
            [
                stage[pl.ds(core * 8 + h, CHIPS, stride=16), :],
                stage[pl.ds(8 - core * 8 + h, CHIPS, stride=16), :],
            ],
            axis=0,
        ).T.astype(bf16)
        lefts += [block[:64], block[64:]]
    v = nn(jnp.concatenate(lefts, axis=1), pick[...])
    v = (v * jnp.where(iota((1, 2048), 1) == 0, 1.0, 2.0)).astype(bf16)
    rights = [None] * 4
    for odd in range(2):
        left = jnp.concatenate(
            [
                v[16 * q : 16 * q + 16, 128 * h : 128 * h + 128]
                for h in range(16)
                for q in (odd, odd + 2)
            ],
            axis=0,
        )
        g = nn(jnp.concatenate([left, left], axis=1), back[odd])
        g = g.reshape(16, 2, 2, 8, 512)
        parts = ([], [])
        for par in range(2):
            at = 256 * par
            g0c, g0s = g[:, :, 0, :, at : at + 128], g[:, :, 0, :, at + 128 : at + 256]
            g1c, g1s = g[:, :, 1, :, at : at + 128], g[:, :, 1, :, at + 128 : at + 256]
            ur, ui = g0c - g1s, g0s + g1c
            tc, ts = unwind[odd, 0, par][:, None], unwind[odd, 1, par][:, None]
            er, ei = ur * tc - ui * ts, ur * ts + ui * tc
            for k in range(2):
                parts[k].append(er[:, k].reshape(128, 128))
                parts[k].append(ei[:, k].reshape(128, 128))
        for k in range(2):
            rights[odd + 2 * k] = jnp.concatenate(parts[k], axis=0)
    for k in range(2):
        high, low = two_parts(jnp.concatenate(rights[2 * k : 2 * k + 2], axis=1))
        sky = nn(last_h[...], high) + nn(last_h[...], low) + nn(last_l[...], high)
        for q in range(2):
            one = sky[:, 128 * q : 128 * q + 128].reshape(2, 4, 32, 128)
            for b in range(NBIN):
                kappa_ref[b, pl.ds(2 * k + q, 32, stride=4), :] = one[0, b]
                potential_ref[b, pl.ds(2 * k + q, 32, stride=4), :] = one[1, b]

    sent(id1.at[pl.ds(0, LOCAL - 1)], 3)
    sent(id2.at[pl.ds(0, BANDS - 1)], 4)
    sent(in1.at[pl.ds(0, DEVICES - 1)], 0)
    sent(near2, 5)
    sent(near3, 6)
    sent(in2.at[pl.ds(0, CHIPS - 1)], 1)
    sent(in3.at[pl.ds(0, CHIPS - 1)], 2)


def per_device(weights, offsets, counts, block_ids, m_table, legendre):
    constants = [jnp.asarray(t) for t in tables()]
    vmem = pl.BlockSpec(memory_space=pltpu.VMEM)
    hbm = pl.BlockSpec(memory_space=pltpu.HBM)
    shape = jax.ShapeDtypeStruct((NBIN, 128, 128), f32)
    kappa, potential = pl.pallas_call(
        kernel,
        out_shape=(pltpu.VMEM(shape.shape, f32),) * 2,
        in_specs=[hbm] * 2 + [vmem] * 3 + [hbm] * 11,
        out_specs=(vmem, vmem),
        scratch_shapes=[
            *[pltpu.VMEM(t.shape, t.dtype) for t in constants],
            pltpu.VMEM((SLOTS, DEGREES, CYCLES), bf16),
            pltpu.VMEM((DEVICES, 32, 128), bf16),
            pltpu.VMEM((DEVICES, 32, 128), bf16),
            pltpu.VMEM((CHIPS, 4, 128), f32),
            pltpu.VMEM((CHIPS, 2, 4, 128), f32),
            pltpu.VMEM((CHIPS, 2, 4, 128), f32),
            pltpu.VMEM((CHIPS * 6, 128), bf16),
            pltpu.VMEM((CHIPS * 6, 128), bf16),
            pltpu.VMEM((CHIPS, 16, 128), bf16),
            pltpu.VMEM((CHIPS, 16, 128), bf16),
            pltpu.VMEM((CHIPS * 16, 128), f32),
            pltpu.VMEM((CAP, DEVICES), f32),
            pltpu.VMEM((LOCAL, CAP, DEVICES), f32),
            pltpu.VMEM((BANDS, 1, 128), f32),
            pltpu.VMEM((BANDS, 1, 128), f32),
            pltpu.VMEM((512, 4096), bf16),
            pltpu.VMEM((SLOTS * 128, 2048), bf16),
            pltpu.VMEM((SLOTS, 16, DEGREES), bf16),
            pltpu.VMEM((SLOTS * 16, CYCLES), bf16),
            pltpu.VMEM((DEVICES, CAP * NBIN, 128), bf16),
            pltpu.VMEM((DEVICES, CAP, 128), jnp.int32),
            pltpu.VMEM((512, 512), bf16),
            pltpu.VMEM((SLOTS * 16, 128), bf16),
            pltpu.VMEM((512, 512), bf16),
            pltpu.VMEM((16, DEGREES), f32),
            pltpu.SemaphoreType.DMA((8,)),
            pltpu.SemaphoreType.DMA((10,)),
            pltpu.SemaphoreType.DMA((SLOTS,)),
            pltpu.SemaphoreType.DMA((7,)),
            pltpu.SemaphoreType.DMA((7,)),
            pltpu.SemaphoreType.DMA((4,)),
        ],
        compiler_params=pltpu.CompilerParams(
            collective_id=0, has_side_effects=True, vmem_limit_bytes=60 << 20
        ),
        name="deposit_filter",
    )(
        weights[0].reshape(DEVICES, CAP * NBIN, 128),
        offsets[0],
        jnp.swapaxes(block_ids, 1, 2).reshape(CAP, DEVICES),
        counts,
        m_table,
        legendre,
        *constants,
    )
    maps = [x.reshape(NBIN, 32, 4, 128).transpose(0, 2, 1, 3) for x in (kappa, potential)]
    return tuple(x.reshape(NBIN, 4, NPHI) for x in maps)


def solution(mesh):
    placed = (
        P(("blk", "ma"), None, None, None, None),
        P(("blk", "ma"), None, None, None),
        P(("blk", "ma"), None),
        P(("blk", "ma"), None, None),
        P(),
        P(("blk", "ma"), None, None),
    )
    return jax.shard_map(
        per_device,
        mesh=mesh,
        in_specs=placed,
        out_specs=(P(None, ("blk", "ma"), None), P(None, ("blk", "ma"), None)),
        check_vma=False,
    )
```
